32 devices in a mesh: section: 4 (over y, x), ctx: 8 (over z, core).
Axes of the slice: x: 2, y: 2, z: 4, core: 2. Of those that a mesh axis runs over, the one named last changes fastest.
Arguments:
- queries: bfloat16 [2, 4, 1024, 1024], P(None, 'section', 'ctx'), may hold values from -8 to 8
- out_grad: bfloat16 [2, 4, 1024, 1024], P(None, 'section', 'ctx'), may hold values from -6 to 6
- keys: bfloat16 [4, 1024, 128], P('section', 'ctx'), may hold values from -4 to 4
- values: bfloat16 [4, 1024, 128], P('section', 'ctx'), may hold values from -6 to 6
- entering_keys: bfloat16 [1024, 128], P('ctx'), may hold values from -4 to 4
- entering_values: bfloat16 [1024, 128], P('ctx'), may hold values from -6 to 6
- key_grads_in: float32 [4, 1024, 128], P('section', 'ctx'), may hold values from -4 to 4
- value_grads_in: float32 [4, 1024, 128], P('section', 'ctx'), may hold values from -4 to 4
- group_order: int32 [8], replicated, may hold values from 0 to 7, each once
Outputs:
- query_grads: bfloat16 [2, 4, 1024, 1024], P(None, 'section', 'ctx')
- key_grads: float32 [2, 4, 1024, 128], P(None, 'section', 'ctx')
- value_grads: float32 [2, 4, 1024, 128], P(None, 'section', 'ctx')
The draws below stay inside these ranges and needn't reach their ends.
Inputs may be any that keep to these rules, and one draw needn't show every extreme that they name: `group_order`: each number 0 to 7 appears once.
All inputs are finite; a program needn't handle non-finite values.
Results may differ from the reference program's by a relative error of at most 0.0062.
Values may be sent and summed in bfloat16 or wider, within the bound.
No kernel may reach another device: no remote copies, remote signals or barrier semaphores. Data moves between devices by JAX's collectives and lax.ppermute only.
A program may use at most 128 MiB of HBM per device.

```python
import jax
import jax.numpy as jnp
from jax import lax

CTX_DEV = 128
HEADS = 8
HEAD_DIM = 128
TICKS = 2
GROUPS = 8
SEQ = 1024
SECTIONS = 4


def key_tables(key):
    normal_part = jax.random.normal(jax.random.fold_in(key, 11), (SECTIONS + 1, SEQ, HEAD_DIM), jnp.float32)
    normal_part = jnp.clip(normal_part, -4.0, 4.0)
    return normal_part


def draw_keys(key, part):
    return key_tables(key)[:SECTIONS].astype(jnp.bfloat16)


def draw_entering_keys(key, part):
    return key_tables(key)[SECTIONS].astype(jnp.bfloat16)


def draw_queries(key, part):
    normal_part = jax.random.normal(jax.random.fold_in(key, 23), (TICKS, SECTIONS, SEQ, HEADS, HEAD_DIM), jnp.float32)
    normal_part = jnp.clip(normal_part, -4.0, 4.0)
    return normal_part.reshape(TICKS, SECTIONS, SEQ, HEADS * HEAD_DIM).astype(jnp.bfloat16)


def block_scale(rng, shape, split, low, top_value):
    def one(axis_at, shards_of):
        steps = jax.random.uniform(jax.random.fold_in(jax.random.fold_in(rng, 6), axis_at), (shards_of,), jnp.float32, low / len(split), top_value / len(split))
        return jnp.repeat(jnp.exp(steps), shape[axis_at] // shards_of).reshape((-1,) + (1,) * (len(shape) - axis_at - 1))

    level = one(*split[0])
    for cut in split[1:]:
        level = level * one(*cut)
    return level


def bell_draw(key, extent, deviation, bound, split=(), kind=jnp.bfloat16):
    loudness = block_scale(key, extent, split, -0.22, 0.18) if split else 1.0
    values = jax.random.normal(key, extent, jnp.float32) * deviation * loudness
    return jnp.minimum(jnp.maximum(values, -bound), bound).astype(kind)


def setup_inputs(seed: int = 0) -> dict:
    key_list = jax.random.split(jax.random.key(seed), 10)
    return {
        "queries": draw_queries(jax.random.fold_in(key_list[9], 71), 0),
        "out_grad": bell_draw(key_list[1], (TICKS, SECTIONS, SEQ, HEADS * HEAD_DIM), 1.0, 6.0, ((1, 4), (2, 8))),
        "keys": draw_keys(jax.random.fold_in(key_list[9], 71), 0),
        "values": bell_draw(key_list[3], (SECTIONS, SEQ, HEAD_DIM), 1.0, 6.0, ((0, 4), (1, 8))),
        "entering_keys": draw_entering_keys(jax.random.fold_in(key_list[9], 71), 0),
        "entering_values": bell_draw(key_list[5], (SEQ, HEAD_DIM), 1.0, 6.0, ((0, 8),)),
        "key_grads_in": bell_draw(key_list[6], (SECTIONS, SEQ, HEAD_DIM), 0.25, 4.0, ((0, 4), (1, 8)), jnp.float32),
        "value_grads_in": bell_draw(key_list[7], (SECTIONS, SEQ, HEAD_DIM), 0.25, 4.0, ((0, 4), (1, 8)), jnp.float32),
        "group_order": jax.random.permutation(key_list[8], GROUPS).astype(jnp.int32),
    }


MASK_FILL = -1e30


def token_positions(group_order):
    row_ids = jnp.arange(SEQ, dtype=jnp.int32)
    return (group_order[row_ids // CTX_DEV] * CTX_DEV + row_ids % CTX_DEV).astype(jnp.int32)


def attend_back(query_all, grad_all, key_block, value_block, positions):
    score_scale = 1.0 / (HEAD_DIM ** 0.5)
    query_heads = query_all.reshape(SEQ, HEADS, HEAD_DIM)
    grad_heads = grad_all.reshape(SEQ, HEADS, HEAD_DIM)
    allowed = positions[None, :] <= positions[:, None]
    query_parts = []
    key_total = jnp.zeros((SEQ, HEAD_DIM), jnp.float32)
    value_total = jnp.zeros((SEQ, HEAD_DIM), jnp.float32)
    for head in range(HEADS):
        scores = jnp.dot(query_heads[:, head], key_block.T, preferred_element_type=jnp.float32) * score_scale
        scores = jnp.where(allowed, scores, MASK_FILL)
        biggest = jnp.max(scores, axis=1, keepdims=True)
        expo = jnp.where(allowed, jnp.exp(scores - biggest), 0.0)
        probs = expo / jnp.sum(expo, axis=1, keepdims=True)
        prob_grads = jnp.dot(grad_heads[:, head], value_block.T, preferred_element_type=jnp.float32)
        deltas = jnp.sum(probs * prob_grads, axis=1, keepdims=True)
        score_grad = (probs * (prob_grads - deltas)).astype(jnp.bfloat16)
        probs_half = probs.astype(jnp.bfloat16)
        query_parts.append((jnp.dot(score_grad, key_block, preferred_element_type=jnp.float32) * score_scale).astype(jnp.bfloat16))
        key_total = key_total + jnp.dot(score_grad.T, query_heads[:, head], preferred_element_type=jnp.float32) * score_scale
        value_total = value_total + jnp.dot(probs_half.T, grad_heads[:, head], preferred_element_type=jnp.float32)
    return jnp.stack(query_parts, axis=1).reshape(SEQ, HEADS * HEAD_DIM), key_total, value_total


def reference(queries, out_grad, keys, values, entering_keys, entering_values, key_grads_in, value_grads_in, group_order):
    positions = token_positions(group_order)

    def section_step(operands):
        query_all, grad_all, key_block, value_block, key_acc, value_acc = operands
        query_grad, key_total, value_total = attend_back(query_all, grad_all, key_block, value_block, positions)
        return query_grad, key_acc + key_total, value_acc + value_total

    first = lax.map(section_step, (queries[0], out_grad[0], keys, values, key_grads_in, value_grads_in))
    next_keys = jnp.concatenate([keys[1:], entering_keys[None]], axis=0)
    next_values = jnp.concatenate([values[1:], entering_values[None]], axis=0)
    next_key_acc = jnp.concatenate([first[1][1:], jnp.zeros_like(first[1][:1])], axis=0)
    next_value_acc = jnp.concatenate([first[2][1:], jnp.zeros_like(first[2][:1])], axis=0)
    second = lax.map(section_step, (queries[1], out_grad[1], next_keys, next_values, next_key_acc, next_value_acc))
    query_grads = jnp.stack([first[0], second[0]], axis=0)
    key_grads = jnp.stack([first[1], second[1]], axis=0)
    value_grads = jnp.stack([first[2], second[2]], axis=0)
    return query_grads, key_grads, value_grads
```

```python
import functools
import math

import jax
import jax.numpy as jnp
from jax import lax
from jax.experimental import pallas as pl
from jax.experimental.pallas import tpu as pltpu
from jax.sharding import PartitionSpec as P

MASK_FILL = -1e30
ROW_BLOCK = 64


def tick_kernel(tick, order_ref, q_ref, g_ref, kv_ref, *rest):
    dq_ref, terms_ref, s_ref, dp_ref, p_ref, ds_ref, acc_ref = rest[-7:]
    local_rows = q_ref.shape[2]
    key_rows = kv_ref.shape[0]
    head_dim = kv_ref.shape[1] // 2
    heads = q_ref.shape[3] // head_dim
    pairs = heads // 2
    width = 2 * local_rows
    scale = 1.0 / math.sqrt(head_dim)
    exp_scale = scale * math.log2(math.e)

    own_group = order_ref[lax.axis_index("ctx")]
    key_mat = kv_ref[:, :head_dim]
    value_mat = kv_ref[:, head_dim:]
    key_t = key_mat.T
    blocks_per_shard = local_rows // ROW_BLOCK
    row_iota = lax.broadcasted_iota(jnp.int32, (ROW_BLOCK, width), 0)
    col_iota = lax.broadcasted_iota(jnp.int32, (ROW_BLOCK, width), 1)
    row_minus_col = row_iota - lax.rem(col_iota, local_rows)

    def stacked(ref, pair):
        lo = 2 * pair * head_dim
        return jnp.concatenate(
            [ref[0, 0, :, lo : lo + head_dim], ref[0, 0, :, lo + head_dim : lo + 2 * head_dim]],
            axis=0,
        )

    blocks = range(key_rows // ROW_BLOCK)
    contract_last = (((1,), (1,)), ((), ()))
    for pair in range(pairs):
        q_pair = stacked(q_ref, pair)
        g_pair = stacked(g_ref, pair)
        s_ref[pair] = lax.dot_general(
            key_mat, q_pair, contract_last, preferred_element_type=jnp.float32
        )
        dp_ref[pair] = lax.dot_general(
            value_mat, g_pair, contract_last, preferred_element_type=jnp.float32
        )
        biggest = jnp.full((8, width), MASK_FILL, jnp.float32)
        for block in blocks:
            rows = slice(block * ROW_BLOCK, (block + 1) * ROW_BLOCK)
            shard, part = divmod(block, blocks_per_shard)
            limit = (own_group - order_ref[shard]) * local_rows - part * ROW_BLOCK
            scores = jnp.where(row_minus_col <= limit, s_ref[pair, rows], MASK_FILL)
            s_ref[pair, rows] = scores
            biggest = jnp.maximum(
                biggest, jnp.max(scores.reshape(ROW_BLOCK // 8, 8, width), axis=0)
            )
        shift = jnp.max(biggest, axis=0, keepdims=True) * exp_scale
        total = jnp.zeros((8, width), jnp.float32)
        weighted = jnp.zeros((8, width), jnp.float32)
        for block in blocks:
            rows = slice(block * ROW_BLOCK, (block + 1) * ROW_BLOCK)
            expo = jnp.exp2(s_ref[pair, rows] * exp_scale - shift)
            s_ref[pair, rows] = expo
            total = total + jnp.sum(expo.reshape(ROW_BLOCK // 8, 8, width), axis=0)
            weighted = weighted + jnp.sum(
                (expo * dp_ref[pair, rows]).reshape(ROW_BLOCK // 8, 8, width), axis=0
            )
        inverse = 1.0 / jnp.sum(total, axis=0, keepdims=True)
        delta = jnp.sum(weighted, axis=0, keepdims=True) * inverse
        for block in blocks:
            rows = slice(block * ROW_BLOCK, (block + 1) * ROW_BLOCK)
            probs = s_ref[pair, rows] * inverse
            p_ref[pair, rows] = probs.astype(jnp.bfloat16)
            ds_ref[pair, rows] = (probs * (dp_ref[pair, rows] - delta)).astype(jnp.bfloat16)
        score_grad = ds_ref[pair]
        key_terms = jnp.dot(score_grad, q_pair, preferred_element_type=jnp.float32)
        value_terms = jnp.dot(p_ref[pair], g_pair, preferred_element_type=jnp.float32)
        if pair == 0:
            acc_ref[:, :head_dim] = key_terms
            acc_ref[:, head_dim:] = value_terms
        elif pair < pairs - 1:
            acc_ref[:, :head_dim] += key_terms
            acc_ref[:, head_dim:] += value_terms
        else:
            terms_ref[:, :head_dim] = ((acc_ref[:, :head_dim] + key_terms) * scale).astype(
                terms_ref.dtype
            )
            terms_ref[:, head_dim:] = (acc_ref[:, head_dim:] + value_terms).astype(terms_ref.dtype)
        query_t = jnp.dot(key_t, score_grad, preferred_element_type=jnp.float32) * scale
        for half in range(2):
            lo = (2 * pair + half) * head_dim
            dq_ref[0, 0, :, lo : lo + head_dim] = query_t[
                :, half * local_rows : (half + 1) * local_rows
            ].T.astype(dq_ref.dtype)


def attend_back(tick, group_order, queries, out_grad, kv, query_grads):
    ticks, _, local_rows, model = queries.shape
    key_rows, width = kv.shape[0], kv.shape[1] // ticks
    head_dim = width // 2
    pairs = model // head_dim // 2
    tick_block = pl.BlockSpec((1, 1, local_rows, model), lambda i: (tick, 0, 0, 0))
    operands = [group_order, queries, out_grad, kv]
    in_specs = [
        pl.BlockSpec(memory_space=pltpu.SMEM),
        tick_block,
        tick_block,
        pl.BlockSpec((key_rows, width), lambda i: (0, tick)),
    ]
    aliases = {}
    if query_grads is not None:
        operands.append(query_grads)
        in_specs.append(pl.BlockSpec(memory_space=pl.ANY))
        aliases = {4: 0}
    tile = (pairs, key_rows, 2 * local_rows)
    return pl.pallas_call(
        functools.partial(tick_kernel, tick),
        grid=(1,),
        out_shape=(
            jax.ShapeDtypeStruct(queries.shape, jnp.bfloat16),
            jax.ShapeDtypeStruct((key_rows, width), jnp.bfloat16),
        ),
        in_specs=in_specs,
        out_specs=(tick_block, pl.BlockSpec((key_rows, width), lambda i: (0, 0))),
        scratch_shapes=[
            pltpu.VMEM(tile, jnp.float32),
            pltpu.VMEM(tile, jnp.float32),
            pltpu.VMEM(tile, jnp.bfloat16),
            pltpu.VMEM(tile, jnp.bfloat16),
            pltpu.VMEM((key_rows, width), jnp.float32),
        ],
        input_output_aliases=aliases,
        compiler_params=pltpu.CompilerParams(vmem_limit_bytes=44 * 2**20),
        cost_estimate=pl.CostEstimate(
            flops=10 * model * key_rows * local_rows,
            bytes_accessed=6 * local_rows * model + 4 * key_rows * width,
            transcendentals=model // head_dim * key_rows * local_rows,
        ),
    )(*operands)


def body(
    queries,
    out_grad,
    keys,
    values,
    entering_keys,
    entering_values,
    key_grads_in,
    value_grads_in,
    group_order,
):
    local_rows, head_dim = keys.shape[1:]
    ctx_count = lax.axis_size("ctx")
    sections = lax.axis_size("section")
    section = lax.axis_index("section")

    own_pair = jnp.concatenate([keys[0], values[0]], axis=1)
    entering_pair = jnp.concatenate([entering_keys, entering_values], axis=1)
    leaving_pair = jnp.where(section == 0, entering_pair, own_pair)
    next_pair = lax.ppermute(
        leaving_pair, "section", [(i, (i - 1) % sections) for i in range(sections)]
    )
    gathered = lax.all_gather(
        jnp.concatenate([own_pair, next_pair], axis=1), "ctx", axis=0, tiled=True
    )

    def reduced(terms):
        pieces = lax.all_to_all(
            terms.reshape(ctx_count, local_rows, 2 * head_dim),
            "ctx",
            split_axis=0,
            concat_axis=0,
            tiled=True,
        )
        return jnp.sum(pieces.astype(jnp.float32), axis=0)

    query_grads, terms = attend_back(0, group_order, queries, out_grad, gathered, None)
    first_acc = jnp.concatenate([key_grads_in[0], value_grads_in[0]], axis=1) + reduced(terms)
    moved_acc = lax.ppermute(first_acc, "section", [(i, i - 1) for i in range(1, sections)])
    query_grads, terms = attend_back(1, group_order, queries, out_grad, gathered, query_grads)
    second_acc = moved_acc + reduced(terms)
    key_grads = jnp.stack([first_acc[:, :head_dim], second_acc[:, :head_dim]], axis=0)[:, None]
    value_grads = jnp.stack([first_acc[:, head_dim:], second_acc[:, head_dim:]], axis=0)[:, None]
    return (query_grads, key_grads, value_grads)


def solution(mesh):
    return jax.shard_map(
        body,
        mesh=mesh,
        in_specs=(
            P(None, "section", "ctx", None),
            P(None, "section", "ctx", None),
            P("section", "ctx", None),
            P("section", "ctx", None),
            P("ctx", None),
            P("ctx", None),
            P("section", "ctx", None),
            P("section", "ctx", None),
            P(),
        ),
        out_specs=(
            P(None, "section", "ctx", None),
            P(None, "section", "ctx", None),
            P(None, "section", "ctx", None),
        ),
        check_vma=False,
    )
```

```python
import math

import jax
import jax.numpy as jnp
from jax import lax
from jax.experimental import pallas as pl
from jax.experimental.pallas import tpu as pltpu
from jax.sharding import PartitionSpec as P

MASK_FILL = -1e30
ROW_BLOCK = 64


def tick_kernel(order_ref, q_ref, g_ref, near_ref, far_ref, *rest):
    dq_ref, near_out_ref, far_out_ref, s_ref, dp_ref, p_ref, ds_ref, acc_ref = rest[-8:]
    local_rows = q_ref.shape[2]
    half_rows = near_ref.shape[0]
    key_rows = 2 * half_rows
    head_dim = near_ref.shape[1] // 2
    heads = q_ref.shape[3] // head_dim
    pairs = heads // 2
    width = 2 * local_rows
    scale = 1.0 / math.sqrt(head_dim)
    exp_scale = scale * math.log2(math.e)

    core = lax.axis_index("core")
    own_group = order_ref[2 * lax.axis_index("z") + core]
    key_mat = jnp.concatenate([near_ref[:, :head_dim], far_ref[:, :head_dim]], axis=0)
    value_mat = jnp.concatenate([near_ref[:, head_dim:], far_ref[:, head_dim:]], axis=0)
    key_t = key_mat.T
    blocks_per_shard = local_rows // ROW_BLOCK
    chips = half_rows // local_rows

    def shard_id(slot):
        if slot < chips:
            return 2 * slot + core
        return 2 * (slot - chips) + 1 - core

    row_iota = lax.broadcasted_iota(jnp.int32, (ROW_BLOCK, width), 0)
    col_iota = lax.broadcasted_iota(jnp.int32, (ROW_BLOCK, width), 1)
    row_minus_col = row_iota - lax.rem(col_iota, local_rows)

    def stacked(ref, pair):
        lo = 2 * pair * head_dim
        return jnp.concatenate(
            [ref[0, 0, :, lo : lo + head_dim], ref[0, 0, :, lo + head_dim : lo + 2 * head_dim]],
            axis=0,
        )

    blocks = range(key_rows // ROW_BLOCK)
    contract_last = (((1,), (1,)), ((), ()))
    for pair in range(pairs):
        q_pair = stacked(q_ref, pair)
        g_pair = stacked(g_ref, pair)
        s_ref[pair] = lax.dot_general(
            key_mat, q_pair, contract_last, preferred_element_type=jnp.float32
        )
        dp_ref[pair] = lax.dot_general(
            value_mat, g_pair, contract_last, preferred_element_type=jnp.float32
        )
        biggest = jnp.full((8, width), MASK_FILL, jnp.float32)
        for block in blocks:
            rows = slice(block * ROW_BLOCK, (block + 1) * ROW_BLOCK)
            shard, part = divmod(block, blocks_per_shard)
            limit = (own_group - order_ref[shard_id(shard)]) * local_rows - part * ROW_BLOCK
            scores = jnp.where(row_minus_col <= limit, s_ref[pair, rows], MASK_FILL)
            s_ref[pair, rows] = scores
            biggest = jnp.maximum(
                biggest, jnp.max(scores.reshape(ROW_BLOCK // 8, 8, width), axis=0)
            )
        shift = jnp.max(biggest, axis=0, keepdims=True) * exp_scale
        total = jnp.zeros((8, width), jnp.float32)
        weighted = jnp.zeros((8, width), jnp.float32)
        for block in blocks:
            rows = slice(block * ROW_BLOCK, (block + 1) * ROW_BLOCK)
            expo = jnp.exp2(s_ref[pair, rows] * exp_scale - shift)
            s_ref[pair, rows] = expo
            total = total + jnp.sum(expo.reshape(ROW_BLOCK // 8, 8, width), axis=0)
            weighted = weighted + jnp.sum(
                (expo * dp_ref[pair, rows]).reshape(ROW_BLOCK // 8, 8, width), axis=0
            )
        inverse = 1.0 / jnp.sum(total, axis=0, keepdims=True)
        delta = jnp.sum(weighted, axis=0, keepdims=True) * inverse
        for block in blocks:
            rows = slice(block * ROW_BLOCK, (block + 1) * ROW_BLOCK)
            probs = s_ref[pair, rows] * inverse
            p_ref[pair, rows] = probs.astype(jnp.bfloat16)
            ds_ref[pair, rows] = (probs * (dp_ref[pair, rows] - delta)).astype(jnp.bfloat16)
        score_grad = ds_ref[pair]
        key_terms = jnp.dot(score_grad, q_pair, preferred_element_type=jnp.float32)
        value_terms = jnp.dot(p_ref[pair], g_pair, preferred_element_type=jnp.float32)
        if pair == 0:
            acc_ref[:, :head_dim] = key_terms
            acc_ref[:, head_dim:] = value_terms
        elif pair < pairs - 1:
            acc_ref[:, :head_dim] += key_terms
            acc_ref[:, head_dim:] += value_terms
        else:
            key_terms = (acc_ref[:, :head_dim] + key_terms) * scale
            value_terms = acc_ref[:, head_dim:] + value_terms
            near_out_ref[:, :head_dim] = key_terms[:half_rows].astype(near_out_ref.dtype)
            near_out_ref[:, head_dim:] = value_terms[:half_rows].astype(near_out_ref.dtype)
            far_out_ref[:, :head_dim] = key_terms[half_rows:].astype(far_out_ref.dtype)
            far_out_ref[:, head_dim:] = value_terms[half_rows:].astype(far_out_ref.dtype)
        query_t = jnp.dot(key_t, score_grad, preferred_element_type=jnp.float32) * scale
        for half in range(2):
            lo = (2 * pair + half) * head_dim
            dq_ref[0, 0, :, lo : lo + head_dim] = query_t[
                :, half * local_rows : (half + 1) * local_rows
            ].T.astype(dq_ref.dtype)


def attend_back(tick, group_order, queries, out_grad, near, far, query_grads):
    local_rows, model = queries.shape[2:]
    half_rows, width = near.shape
    key_rows = 2 * half_rows
    head_dim = width // 2
    pairs = model // head_dim // 2
    tick_block = pl.BlockSpec((1, 1, local_rows, model), lambda i: (tick, 0, 0, 0))
    half_block = pl.BlockSpec((half_rows, width), lambda i: (0, 0))
    operands = [group_order, queries, out_grad, near, far]
    in_specs = [
        pl.BlockSpec(memory_space=pltpu.SMEM),
        tick_block,
        tick_block,
        half_block,
        half_block,
    ]
    aliases = {}
    if query_grads is not None:
        aliases = {len(operands): 0}
        operands.append(query_grads)
        in_specs.append(pl.BlockSpec(memory_space=pl.ANY))
    tile = (pairs, key_rows, 2 * local_rows)
    return pl.pallas_call(
        tick_kernel,
        grid=(1,),
        out_shape=(
            jax.ShapeDtypeStruct(queries.shape, jnp.bfloat16),
            jax.ShapeDtypeStruct((half_rows, width), jnp.float32),
            jax.ShapeDtypeStruct((half_rows, width), jnp.bfloat16),
        ),
        in_specs=in_specs,
        out_specs=(tick_block, half_block, half_block),
        scratch_shapes=[
            pltpu.VMEM(tile, jnp.float32),
            pltpu.VMEM(tile, jnp.float32),
            pltpu.VMEM(tile, jnp.bfloat16),
            pltpu.VMEM(tile, jnp.bfloat16),
            pltpu.VMEM((key_rows, width), jnp.float32),
        ],
        input_output_aliases=aliases,
        compiler_params=pltpu.CompilerParams(vmem_limit_bytes=44 * 2**20),
        cost_estimate=pl.CostEstimate(
            flops=10 * model * key_rows * local_rows,
            bytes_accessed=6 * local_rows * model + 5 * key_rows * width,
            transcendentals=model // head_dim * key_rows * local_rows,
        ),
    )(*operands)


def other_core(block):
    return lax.ppermute(block, "core", [(0, 1), (1, 0)])


def along_chips(blocks):
    return lax.all_to_all(blocks, "z", split_axis=0, concat_axis=0, tiled=True)


def body(
    queries,
    out_grad,
    keys,
    values,
    entering_keys,
    entering_values,
    key_grads_in,
    value_grads_in,
    group_order,
):
    local_rows, head_dim = keys.shape[1:]
    width = 2 * head_dim
    chips = lax.axis_size("z")
    sections = lax.axis_size("section")
    section = lax.axis_index("section")

    own_pair = jnp.concatenate([keys[0], values[0]], axis=1)
    entering_pair = jnp.concatenate([entering_keys, entering_values], axis=1)
    leaving_pair = jnp.where(section == 0, entering_pair, own_pair)
    next_pair = lax.ppermute(
        leaving_pair, "section", [(i, (i - 1) % sections) for i in range(sections)]
    )

    def gathered(pair):
        near = along_chips(jnp.broadcast_to(pair, (chips, local_rows, width)))
        near = near.reshape(chips * local_rows, width)
        return near, other_core(near)

    def reduced(near_terms, far_terms):
        chip_terms = near_terms + other_core(far_terms).astype(jnp.float32)
        pieces = along_chips(
            chip_terms.astype(jnp.bfloat16).reshape(chips, local_rows, width)
        )
        return jnp.sum(pieces.astype(jnp.float32), axis=0)

    first_kv = gathered(own_pair)
    second_kv = gathered(next_pair)
    query_grads, near, far = attend_back(0, group_order, queries, out_grad, *first_kv, None)
    first_acc = jnp.concatenate([key_grads_in[0], value_grads_in[0]], axis=1) + reduced(near, far)
    moved_acc = lax.ppermute(first_acc, "section", [(i, i - 1) for i in range(1, sections)])
    query_grads, near, far = attend_back(
        1, group_order, queries, out_grad, *second_kv, query_grads
    )
    second_acc = moved_acc + reduced(near, far)
    key_grads = jnp.stack([first_acc[:, :head_dim], second_acc[:, :head_dim]], axis=0)[:, None]
    value_grads = jnp.stack([first_acc[:, head_dim:], second_acc[:, head_dim:]], axis=0)[:, None]
    return (query_grads, key_grads, value_grads)


def solution(mesh):
    sections, ctx_count = mesh.shape["section"], mesh.shape["ctx"]
    chip_mesh = jax.sharding.Mesh(
        mesh.devices.reshape(sections, ctx_count // 2, 2), ("section", "z", "core")
    )
    tokens = ("z", "core")
    return jax.shard_map(
        body,
        mesh=chip_mesh,
        in_specs=(
            P(None, "section", tokens, None),
            P(None, "section", tokens, None),
            P("section", tokens, None),
            P("section", tokens, None),
            P(tokens, None),
            P(tokens, None),
            P("section", tokens, None),
            P("section", tokens, None),
            P(),
        ),
        out_specs=(
            P(None, "section", tokens, None),
            P(None, "section", tokens, None),
            P(None, "section", tokens, None),
        ),
        check_vma=False,
    )
```

```python
import math

import jax
import jax.numpy as jnp
from jax import lax
from jax.experimental import pallas as pl
from jax.experimental.pallas import tpu as pltpu
from jax.sharding import PartitionSpec as P

MASK_FILL = -1e30
CONTRACT_LAST = (((1,), (1,)), ((), ()))


def tick_kernel(blocks, aliased, *refs):
    order_ref, q_ref, g_ref = refs[:3]
    kv_refs = refs[3 : 3 + blocks]
    outs = refs[3 + blocks + aliased :]
    dq_ref = outs[0]
    term_refs = outs[1 : 1 + blocks]
    e_ref, dp_ref, p_ref, ds_ref, acc_ref, kt_ref = outs[1 + blocks :]
    local_rows, head_dim = kv_refs[0].shape[0], kv_refs[0].shape[1] // 2
    heads = q_ref.shape[3] // head_dim
    pairs = heads // 2
    width = 2 * local_rows
    chips = blocks // 2
    scale = 1.0 / math.sqrt(head_dim)
    exp_scale = scale * math.log2(math.e)

    core = lax.axis_index("core")
    chip = lax.axis_index("z")
    own_group = order_ref[2 * chip + core]
    limits = []
    for slot in range(blocks):
        source = lax.rem(chip + chips - slot % chips, chips)
        parity = core if slot < chips else 1 - core
        limits.append((own_group - order_ref[2 * source + parity]) * local_rows)
    row_minus_col = lax.broadcasted_iota(jnp.int32, (local_rows, width), 0) - lax.rem(
        lax.broadcasted_iota(jnp.int32, (local_rows, width), 1), local_rows
    )
    for slot in range(blocks):
        kt_ref[:, slot * local_rows : (slot + 1) * local_rows] = kv_refs[slot][:, :head_dim].T

    def stacked(ref, pair):
        lo = 2 * pair * head_dim
        return jnp.concatenate(
            [ref[0, 0, :, lo : lo + head_dim], ref[0, 0, :, lo + head_dim : lo + 2 * head_dim]],
            axis=0,
        )

    def rows_of(slot):
        return slice(slot * local_rows, (slot + 1) * local_rows)

    for pair in range(pairs):
        q_pair = stacked(q_ref, pair)
        g_pair = stacked(g_ref, pair)
        peaks, totals, weights = [], [], []
        for slot in range(blocks):
            scores = lax.dot_general(
                kv_refs[slot][:, :head_dim],
                q_pair,
                CONTRACT_LAST,
                preferred_element_type=jnp.float32,
            )
            scores = jnp.where(row_minus_col <= limits[slot], scores, MASK_FILL)
            peak = jnp.max(scores, axis=0, keepdims=True) * exp_scale
            expo = jnp.exp2(scores * exp_scale - peak)
            prob_grads = lax.dot_general(
                kv_refs[slot][:, head_dim:],
                g_pair,
                CONTRACT_LAST,
                preferred_element_type=jnp.float32,
            )
            e_ref[pair, rows_of(slot)] = expo
            dp_ref[pair, rows_of(slot)] = prob_grads
            peaks.append(peak)
            totals.append(jnp.sum(expo, axis=0, keepdims=True))
            weights.append(jnp.sum(expo * prob_grads, axis=0, keepdims=True))
        biggest = peaks[0]
        for peak in peaks[1:]:
            biggest = jnp.maximum(biggest, peak)
        factors = [jnp.exp2(peak - biggest) for peak in peaks]
        total = sum(part * factor for part, factor in zip(totals, factors))
        weighted = sum(part * factor for part, factor in zip(weights, factors))
        inverse = 1.0 / total
        delta = weighted * inverse
        for slot in range(blocks):
            probs = e_ref[pair, rows_of(slot)] * (factors[slot] * inverse)
            p_ref[pair, rows_of(slot)] = probs.astype(jnp.bfloat16)
            ds_ref[pair, rows_of(slot)] = (
                probs * (dp_ref[pair, rows_of(slot)] - delta)
            ).astype(jnp.bfloat16)
        score_grad = ds_ref[pair]
        key_terms = jnp.dot(score_grad, q_pair, preferred_element_type=jnp.float32)
        value_terms = jnp.dot(p_ref[pair], g_pair, preferred_element_type=jnp.float32)
        if pair > 0:
            key_terms += acc_ref[:, :head_dim]
            value_terms += acc_ref[:, head_dim:]
        if pair < pairs - 1:
            acc_ref[:, :head_dim] = key_terms
            acc_ref[:, head_dim:] = value_terms
        else:
            for slot, out in enumerate(term_refs):
                out[:, :head_dim] = (key_terms[rows_of(slot)] * scale).astype(out.dtype)
                out[:, head_dim:] = value_terms[rows_of(slot)].astype(out.dtype)
        query_t = jnp.dot(kt_ref[...], score_grad, preferred_element_type=jnp.float32) * scale
        for half in range(2):
            lo = (2 * pair + half) * head_dim
            dq_ref[0, 0, :, lo : lo + head_dim] = query_t[
                :, half * local_rows : (half + 1) * local_rows
            ].T.astype(dq_ref.dtype)


def attend_back(tick, group_order, queries, out_grad, near, far, query_grads):
    local_rows, model = queries.shape[2:]
    kv_blocks = [*near, *far]
    blocks = len(kv_blocks)
    width = kv_blocks[0].shape[1]
    key_rows = blocks * local_rows
    head_dim = width // 2
    pairs = model // head_dim // 2
    tick_block = pl.BlockSpec((1, 1, local_rows, model), lambda i: (tick, 0, 0, 0))
    shard_block = pl.BlockSpec((local_rows, width), lambda i: (0, 0))
    operands = [group_order, queries, out_grad, *kv_blocks]
    in_specs = [
        pl.BlockSpec(memory_space=pltpu.SMEM),
        tick_block,
        tick_block,
        *[shard_block] * blocks,
    ]
    aliases = {}
    if query_grads is not None:
        aliases = {len(operands): 0}
        operands.append(query_grads)
        in_specs.append(pl.BlockSpec(memory_space=pl.ANY))
    tile = (pairs, key_rows, 2 * local_rows)

    def kernel(*refs):
        tick_kernel(blocks, len(aliases), *refs)

    kinds = [jnp.float32] * len(near) + [jnp.bfloat16] * len(far)
    query_grads, *terms = pl.pallas_call(
        kernel,
        grid=(1,),
        out_shape=(
            jax.ShapeDtypeStruct(queries.shape, jnp.bfloat16),
            *[jax.ShapeDtypeStruct((local_rows, width), kind) for kind in kinds],
        ),
        in_specs=in_specs,
        out_specs=(tick_block, *[shard_block] * blocks),
        scratch_shapes=[
            pltpu.VMEM(tile, jnp.float32),
            pltpu.VMEM(tile, jnp.float32),
            pltpu.VMEM(tile, jnp.bfloat16),
            pltpu.VMEM(tile, jnp.bfloat16),
            pltpu.VMEM((key_rows, width), jnp.float32),
            pltpu.VMEM((head_dim, key_rows), jnp.bfloat16),
        ],
        input_output_aliases=aliases,
        compiler_params=pltpu.CompilerParams(vmem_limit_bytes=44 * 2**20),
        cost_estimate=pl.CostEstimate(
            flops=40 * model * key_rows * local_rows,
            bytes_accessed=6 * local_rows * model + 5 * key_rows * width,
            transcendentals=model // head_dim * key_rows * local_rows,
        ),
    )(*operands)
    return query_grads, terms[: len(near)], terms[len(near) :]


def other_core(block):
    return lax.ppermute(block, "core", [(0, 1), (1, 0)])


def along_chips(block, distance):
    chips = lax.axis_size("z")
    route = [(chip, (chip + distance) % chips) for chip in range(chips)]
    return lax.ppermute(block, "z", route)


def section_back(block, distance):
    chips = lax.axis_size("z")
    sections = lax.axis_size("section")
    route = [
        (s * chips + chip, (s - 1) % sections * chips + (chip + distance) % chips)
        for s in range(sections)
        for chip in range(chips)
    ]
    return lax.ppermute(block, ("section", "z"), route)


def body(
    queries,
    out_grad,
    keys,
    values,
    entering_keys,
    entering_values,
    key_grads_in,
    value_grads_in,
    group_order,
):
    head_dim = keys.shape[2]
    chips = lax.axis_size("z")
    sections = lax.axis_size("section")
    section = lax.axis_index("section")

    own_pair = jnp.concatenate([keys[0], values[0]], axis=1)
    entering_pair = jnp.concatenate([entering_keys, entering_values], axis=1)
    leaving_pair = jnp.where(section == 0, entering_pair, own_pair)

    near = [own_pair] + [along_chips(own_pair, k) for k in range(1, chips)]
    far = [other_core(block) for block in near]
    next_near = [section_back(leaving_pair, k) for k in range(chips)]
    query_grads, near_terms, far_terms = attend_back(
        0, group_order, queries, out_grad, near, far, None
    )
    query_grads, far_terms, next_near = lax.optimization_barrier(
        (query_grads, far_terms, next_near)
    )
    next_far = [other_core(block) for block in next_near]

    def chip_sums(near_terms, far_terms):
        sums = [
            mine + other_core(theirs).astype(jnp.float32)
            for mine, theirs in zip(near_terms, far_terms)
        ]
        return sums[0], [block.astype(jnp.bfloat16) for block in sums[1:]]

    def reduced(own_sum, leaving):
        for k, block in enumerate(leaving, 1):
            own_sum = own_sum + along_chips(block, -k).astype(jnp.float32)
        return own_sum

    own_sum, leaving = chip_sums(near_terms, far_terms)
    query_grads, leaving = lax.optimization_barrier((query_grads, leaving))
    first_acc = jnp.concatenate([key_grads_in[0], value_grads_in[0]], axis=1) + reduced(
        own_sum, leaving
    )
    moved_acc = lax.ppermute(first_acc, "section", [(i, i - 1) for i in range(1, sections)])
    query_grads, near_terms, far_terms = attend_back(
        1, group_order, queries, out_grad, next_near, next_far, query_grads
    )
    second_acc = moved_acc + reduced(*chip_sums(near_terms, far_terms))
    key_grads = jnp.stack([first_acc[:, :head_dim], second_acc[:, :head_dim]], axis=0)[:, None]
    value_grads = jnp.stack([first_acc[:, head_dim:], second_acc[:, head_dim:]], axis=0)[:, None]
    return (query_grads, key_grads, value_grads)


def solution(mesh):
    sections, ctx_count = mesh.shape["section"], mesh.shape["ctx"]
    chip_mesh = jax.sharding.Mesh(
        mesh.devices.reshape(sections, ctx_count // 2, 2), ("section", "z", "core")
    )
    tokens = ("z", "core")
    return jax.shard_map(
        body,
        mesh=chip_mesh,
        in_specs=(
            P(None, "section", tokens, None),
            P(None, "section", tokens, None),
            P("section", tokens, None),
            P("section", tokens, None),
            P(tokens, None),
            P(tokens, None),
            P("section", tokens, None),
            P("section", tokens, None),
            P(),
        ),
        out_specs=(
            P(None, "section", tokens, None),
            P(None, "section", tokens, None),
            P(None, "section", tokens, None),
        ),
        check_vma=False,
    )
```

```python
import math

import jax
import jax.numpy as jnp
from jax import lax
from jax.experimental import pallas as pl
from jax.experimental.pallas import tpu as pltpu
from jax.sharding import PartitionSpec as P

MASK_FILL = -1e30
CONTRACT_LAST = (((1,), (1,)), ((), ()))


def stack_kernel(q_ref, g_ref, q_out_ref, g_out_ref):
    ticks, _, local_rows, model = q_ref.shape
    head_dim = q_out_ref.shape[1]
    heads = model // head_dim
    for tick in range(ticks):
        for head in range(heads):
            rows = pl.ds((tick * heads + head) * local_rows, local_rows)
            cols = pl.ds(head * head_dim, head_dim)
            q_out_ref[rows, :] = q_ref[tick, 0, :, cols]
            g_out_ref[rows, :] = g_ref[tick, 0, :, cols]


def stacked_heads(queries, out_grad, head_dim):
    rows = queries.size // head_dim
    in_vmem = pl.BlockSpec(memory_space=pltpu.VMEM)
    return pl.pallas_call(
        stack_kernel,
        out_shape=(jax.ShapeDtypeStruct((rows, head_dim), queries.dtype),) * 2,
        in_specs=[in_vmem, in_vmem],
        out_specs=(in_vmem, in_vmem),
        compiler_params=pltpu.CompilerParams(vmem_limit_bytes=8 * 2**20),
        cost_estimate=pl.CostEstimate(
            flops=queries.size, bytes_accessed=8 * queries.size, transcendentals=0
        ),
    )(queries, out_grad)


def tick_kernel(tick, blocks, aliased, *refs):
    order_ref, q_ref, g_ref = refs[:3]
    kv_refs = refs[3 : 3 + blocks]
    outs = refs[3 + blocks + aliased :]
    dq_ref = outs[0]
    term_refs = outs[1 : 1 + blocks]
    e_ref, dp_ref, p_ref, ds_ref, acc_ref, kt_ref, dq_held, dq_sem = outs[1 + blocks :]
    local_rows, head_dim = kv_refs[0].shape[0], kv_refs[0].shape[1] // 2
    heads = dq_held.shape[1] // head_dim
    pairs = heads // 2
    width = 2 * local_rows
    chips = blocks // 2
    scale = 1.0 / math.sqrt(head_dim)
    exp_scale = scale * math.log2(math.e)

    core = lax.axis_index("core")
    chip = lax.axis_index("z")
    own_group = order_ref[2 * chip + core]

    def allowed(slot):
        source = jnp.bitwise_xor(chip, slot % chips)
        parity = core if slot < chips else 1 - core
        return order_ref[2 * source + parity] < own_group

    for slot in range(blocks):
        kt_ref[:, slot * local_rows : (slot + 1) * local_rows] = kv_refs[slot][:, :head_dim].T

    def pair_of(ref, pair):
        return ref[pl.ds((tick * pairs + pair) * width, width), :]

    def rows_of(slot):
        return slice(slot * local_rows, (slot + 1) * local_rows)

    def front(pair):
        q_pair = pair_of(q_ref, pair)
        g_pair = pair_of(g_ref, pair)
        peaks, totals, weights = [], [], []
        for slot in range(blocks):
            scores = lax.dot_general(
                kv_refs[slot][:, :head_dim],
                q_pair,
                CONTRACT_LAST,
                preferred_element_type=jnp.float32,
            )
            if slot == 0:
                key_row = lax.broadcasted_iota(jnp.int32, (local_rows, width), 0)
                query_row = lax.rem(
                    lax.broadcasted_iota(jnp.int32, (local_rows, width), 1), local_rows
                )
                scores = jnp.where(key_row <= query_row, scores, MASK_FILL)
            peak = jnp.max(scores, axis=0, keepdims=True) * exp_scale
            expo = jnp.exp2(scores * exp_scale - peak)
            prob_grads = lax.dot_general(
                kv_refs[slot][:, head_dim:],
                g_pair,
                CONTRACT_LAST,
                preferred_element_type=jnp.float32,
            )
            e_ref[pair, rows_of(slot)] = expo
            dp_ref[pair, rows_of(slot)] = prob_grads
            peaks.append(peak if slot == 0 else jnp.where(allowed(slot), peak, MASK_FILL))
            totals.append(jnp.sum(expo, axis=0, keepdims=True))
            weights.append(jnp.sum(expo * prob_grads, axis=0, keepdims=True))
        biggest = peaks[0]
        for peak in peaks[1:]:
            biggest = jnp.maximum(biggest, peak)
        factors = [jnp.exp2(peak - biggest) for peak in peaks]
        total = sum(part * factor for part, factor in zip(totals, factors))
        weighted = sum(part * factor for part, factor in zip(weights, factors))
        inverse = 1.0 / total
        return [factor * inverse for factor in factors], weighted * inverse

    def back(pair, factors, delta):
        q_pair = pair_of(q_ref, pair)
        g_pair = pair_of(g_ref, pair)
        for slot in range(blocks):
            probs = e_ref[pair, rows_of(slot)] * factors[slot]
            p_ref[pair, rows_of(slot)] = probs.astype(jnp.bfloat16)
            ds_ref[pair, rows_of(slot)] = (
                probs * (dp_ref[pair, rows_of(slot)] - delta)
            ).astype(jnp.bfloat16)
        score_grad = ds_ref[pair]
        key_terms = jnp.dot(score_grad, q_pair, preferred_element_type=jnp.float32)
        value_terms = jnp.dot(p_ref[pair], g_pair, preferred_element_type=jnp.float32)
        if pair > 0:
            key_terms += acc_ref[:, :head_dim]
            value_terms += acc_ref[:, head_dim:]
        if pair < pairs - 1:
            acc_ref[:, :head_dim] = key_terms
            acc_ref[:, head_dim:] = value_terms
        else:
            for slot, out in enumerate(term_refs):
                out[:, :head_dim] = (key_terms[rows_of(slot)] * scale).astype(out.dtype)
                out[:, head_dim:] = value_terms[rows_of(slot)].astype(out.dtype)
        query_t = jnp.dot(kt_ref[...], score_grad, preferred_element_type=jnp.float32) * scale
        for half in range(2):
            lo = (2 * pair + half) * head_dim
            dq_held[:, lo : lo + head_dim] = query_t[
                :, half * local_rows : (half + 1) * local_rows
            ].T.astype(dq_held.dtype)
        cols = pl.ds(2 * pair * head_dim, 2 * head_dim)
        copy = pltpu.make_async_copy(
            dq_held.at[:, cols], dq_ref.at[tick, 0, :, cols], dq_sem.at[pair]
        )
        copy.start()
        return copy

    copies = []
    held = front(0)
    for pair in range(pairs):
        following = front(pair + 1) if pair + 1 < pairs else None
        copies.append(back(pair, *held))
        held = following
    for copy in copies:
        copy.wait()


def attend_back(tick, group_order, queries, q_stack, g_stack, near, far, query_grads):
    local_rows, model = queries.shape[2:]
    kv_blocks = [*near, *far]
    blocks = len(kv_blocks)
    width = kv_blocks[0].shape[1]
    key_rows = blocks * local_rows
    head_dim = width // 2
    pairs = model // head_dim // 2
    in_vmem = pl.BlockSpec(memory_space=pltpu.VMEM)
    operands = [group_order, q_stack, g_stack, *kv_blocks]
    in_specs = [pl.BlockSpec(memory_space=pltpu.SMEM), *[in_vmem] * (2 + blocks)]
    aliases = {}
    if query_grads is not None:
        aliases = {len(operands): 0}
        operands.append(query_grads)
        in_specs.append(pl.BlockSpec(memory_space=pl.ANY))
    tile = (pairs, key_rows, 2 * local_rows)

    def kernel(*refs):
        tick_kernel(tick, blocks, len(aliases), *refs)

    kinds = [jnp.float32] * len(near) + [jnp.bfloat16] * len(far)
    query_grads, *terms = pl.pallas_call(
        kernel,
        out_shape=(
            jax.ShapeDtypeStruct(queries.shape, jnp.bfloat16),
            *[jax.ShapeDtypeStruct((local_rows, width), kind) for kind in kinds],
        ),
        in_specs=in_specs,
        out_specs=(pl.BlockSpec(memory_space=pl.ANY), *[in_vmem] * blocks),
        scratch_shapes=[
            pltpu.VMEM(tile, jnp.float32),
            pltpu.VMEM(tile, jnp.float32),
            pltpu.VMEM(tile, jnp.bfloat16),
            pltpu.VMEM(tile, jnp.bfloat16),
            pltpu.VMEM((key_rows, width), jnp.float32),
            pltpu.VMEM((head_dim, key_rows), jnp.bfloat16),
            pltpu.VMEM((local_rows, model), jnp.bfloat16),
            pltpu.SemaphoreType.DMA((pairs,)),
        ],
        input_output_aliases=aliases,
        compiler_params=pltpu.CompilerParams(vmem_limit_bytes=44 * 2**20),
        cost_estimate=pl.CostEstimate(
            flops=40 * model * key_rows * local_rows,
            bytes_accessed=6 * local_rows * model + 5 * key_rows * width,
            transcendentals=model // head_dim * key_rows * local_rows,
        ),
    )(*operands)
    return query_grads, terms[: len(near)], terms[len(near) :]


def other_core(block):
    return lax.ppermute(block, "core", [(0, 1), (1, 0)])


def across_chips(block, k):
    return lax.ppermute(block, "z", [(chip, chip ^ k) for chip in range(lax.axis_size("z"))])


def body(
    queries,
    out_grad,
    keys,
    values,
    entering_keys,
    entering_values,
    key_grads_in,
    value_grads_in,
    group_order,
):
    head_dim = keys.shape[2]
    chips = lax.axis_size("z")
    sections = lax.axis_size("section")
    section = lax.axis_index("section")

    own_pair = jnp.concatenate([keys[0], values[0]], axis=1)
    entering_pair = jnp.concatenate([entering_keys, entering_values], axis=1)
    leaving_pair = jnp.where(section == 0, entering_pair, own_pair)

    near = [across_chips(own_pair, k) for k in range(1, chips)]
    own_far = other_core(own_pair)
    next_pair = lax.ppermute(
        leaving_pair, "section", [(i, (i - 1) % sections) for i in range(sections)]
    )
    stacks = stacked_heads(queries, out_grad, head_dim)
    near, next_pair, stacks = lax.optimization_barrier((near, next_pair, stacks))
    far = [own_far] + [other_core(block) for block in near]
    next_near = [next_pair] + [across_chips(next_pair, k) for k in range(1, chips)]
    query_grads, near_terms, far_terms = attend_back(
        0, group_order, queries, *stacks, [own_pair, *near], far, None
    )
    query_grads, far_terms, next_near = lax.optimization_barrier(
        (query_grads, far_terms, next_near)
    )
    next_far = [other_core(block) for block in next_near]

    def chip_sums(near_terms, far_terms):
        sums = [
            mine + other_core(theirs).astype(jnp.float32)
            for mine, theirs in zip(near_terms, far_terms)
        ]
        return sums[0], [block.astype(jnp.bfloat16) for block in sums[1:]]

    def reduced(own_sum, leaving):
        for k, block in enumerate(leaving, 1):
            own_sum = own_sum + across_chips(block, k).astype(jnp.float32)
        return own_sum

    own_sum, leaving = chip_sums(near_terms, far_terms)
    query_grads, leaving = lax.optimization_barrier((query_grads, leaving))
    first_acc = jnp.concatenate([key_grads_in[0], value_grads_in[0]], axis=1) + reduced(
        own_sum, leaving
    )
    query_grads, near_terms, far_terms = attend_back(
        1, group_order, queries, *stacks, next_near, next_far, query_grads
    )
    first_acc, far_terms = lax.optimization_barrier((first_acc, far_terms))
    own_sum, leaving = chip_sums(near_terms, far_terms)
    first_acc, leaving = lax.optimization_barrier((first_acc, leaving))
    moved_acc = lax.ppermute(first_acc, "section", [(i, i - 1) for i in range(1, sections)])
    second_acc = moved_acc + reduced(own_sum, leaving)
    key_grads = jnp.stack([first_acc[:, :head_dim], second_acc[:, :head_dim]], axis=0)[:, None]
    value_grads = jnp.stack([first_acc[:, head_dim:], second_acc[:, head_dim:]], axis=0)[:, None]
    return (query_grads, key_grads, value_grads)


def solution(mesh):
    sections, ctx_count = mesh.shape["section"], mesh.shape["ctx"]
    chip_mesh = jax.sharding.Mesh(
        mesh.devices.reshape(sections, ctx_count // 2, 2), ("section", "z", "core")
    )
    tokens = ("z", "core")
    return jax.shard_map(
        body,
        mesh=chip_mesh,
        in_specs=(
            P(None, "section", tokens, None),
            P(None, "section", tokens, None),
            P("section", tokens, None),
            P("section", tokens, None),
            P(tokens, None),
            P(tokens, None),
            P("section", tokens, None),
            P("section", tokens, None),
            P(),
        ),
        out_specs=(
            P(None, "section", tokens, None),
            P(None, "section", tokens, None),
            P(None, "section", tokens, None),
        ),
        check_vma=False,
    )
```

```python
import math

import jax
import jax.numpy as jnp
from jax import lax
from jax.experimental import pallas as pl
from jax.experimental.pallas import tpu as pltpu
from jax.sharding import PartitionSpec as P

MASK_FILL = -1e30
CONTRACT_LAST = (((1,), (1,)), ((), ()))


def stack_kernel(q_ref, g_ref, q_out_ref, g_out_ref):
    ticks, _, local_rows, model = q_ref.shape
    head_dim = q_out_ref.shape[1]
    heads = model // head_dim
    for tick in range(ticks):
        for head in range(heads):
            rows = pl.ds((tick * heads + head) * local_rows, local_rows)
            cols = pl.ds(head * head_dim, head_dim)
            q_out_ref[rows, :] = q_ref[tick, 0, :, cols]
            g_out_ref[rows, :] = g_ref[tick, 0, :, cols]


def stacked_heads(queries, out_grad, head_dim):
    rows = queries.size // head_dim
    in_vmem = pl.BlockSpec(memory_space=pltpu.VMEM)
    return pl.pallas_call(
        stack_kernel,
        out_shape=(jax.ShapeDtypeStruct((rows, head_dim), queries.dtype),) * 2,
        in_specs=[in_vmem, in_vmem],
        out_specs=(in_vmem, in_vmem),
        compiler_params=pltpu.CompilerParams(vmem_limit_bytes=8 * 2**20),
        cost_estimate=pl.CostEstimate(
            flops=queries.size, bytes_accessed=8 * queries.size, transcendentals=0
        ),
    )(queries, out_grad)


def tick_kernel(tick, arrays, aliased, *refs):
    order_ref, q_ref, g_ref = refs[:3]
    outs = refs[3 + arrays + aliased :]
    dq_ref, near_out_ref, far_out_ref = outs[:3]
    e_ref, dp_ref, p_ref, ds_ref, acc_ref, kt_ref, dq_held, dq_sem = outs[3:]
    local_rows, model = dq_held.shape
    head_dim = near_out_ref.shape[1] // 2
    half_rows = near_out_ref.shape[0]
    kv_refs = [
        ref.at[pl.ds(row, local_rows)]
        for ref in refs[3 : 3 + arrays]
        for row in range(0, ref.shape[0], local_rows)
    ]
    blocks = len(kv_refs)
    heads = model // head_dim
    pairs = heads // 2
    width = 2 * local_rows
    chips = blocks // 2
    scale = 1.0 / math.sqrt(head_dim)
    exp_scale = scale * math.log2(math.e)

    core = lax.axis_index("core")
    chip = lax.axis_index("z")
    own_group = order_ref[2 * chip + core]

    def allowed(slot):
        source = jnp.bitwise_xor(chip, slot % chips)
        parity = core if slot < chips else 1 - core
        return order_ref[2 * source + parity] < own_group

    for slot in range(blocks):
        kt_ref[:, slot * local_rows : (slot + 1) * local_rows] = kv_refs[slot][:, :head_dim].T

    def pair_of(ref, pair):
        return ref[pl.ds((tick * pairs + pair) * width, width), :]

    def rows_of(slot):
        return slice(slot * local_rows, (slot + 1) * local_rows)

    def front(pair):
        q_pair = pair_of(q_ref, pair)
        g_pair = pair_of(g_ref, pair)
        peaks, totals, weights = [], [], []
        for slot in range(blocks):
            scores = lax.dot_general(
                kv_refs[slot][:, :head_dim],
                q_pair,
                CONTRACT_LAST,
                preferred_element_type=jnp.float32,
            )
            if slot == 0:
                key_row = lax.broadcasted_iota(jnp.int32, (local_rows, width), 0)
                query_row = lax.rem(
                    lax.broadcasted_iota(jnp.int32, (local_rows, width), 1), local_rows
                )
                scores = jnp.where(key_row <= query_row, scores, MASK_FILL)
            peak = jnp.max(scores, axis=0, keepdims=True) * exp_scale
            expo = jnp.exp2(scores * exp_scale - peak)
            prob_grads = lax.dot_general(
                kv_refs[slot][:, head_dim:],
                g_pair,
                CONTRACT_LAST,
                preferred_element_type=jnp.float32,
            )
            e_ref[pair, rows_of(slot)] = expo
            dp_ref[pair, rows_of(slot)] = prob_grads
            peaks.append(peak if slot == 0 else jnp.where(allowed(slot), peak, MASK_FILL))
            totals.append(jnp.sum(expo, axis=0, keepdims=True))
            weights.append(jnp.sum(expo * prob_grads, axis=0, keepdims=True))
        biggest = peaks[0]
        for peak in peaks[1:]:
            biggest = jnp.maximum(biggest, peak)
        factors = [jnp.exp2(peak - biggest) for peak in peaks]
        total = sum(part * factor for part, factor in zip(totals, factors))
        weighted = sum(part * factor for part, factor in zip(weights, factors))
        inverse = 1.0 / total
        return [factor * inverse for factor in factors], weighted * inverse

    def back(pair, factors, delta):
        q_pair = pair_of(q_ref, pair)
        g_pair = pair_of(g_ref, pair)
        for slot in range(blocks):
            probs = e_ref[pair, rows_of(slot)] * factors[slot]
            p_ref[pair, rows_of(slot)] = probs.astype(jnp.bfloat16)
            ds_ref[pair, rows_of(slot)] = (
                probs * (dp_ref[pair, rows_of(slot)] - delta)
            ).astype(jnp.bfloat16)
        score_grad = ds_ref[pair]
        key_terms = jnp.dot(score_grad, q_pair, preferred_element_type=jnp.float32)
        value_terms = jnp.dot(p_ref[pair], g_pair, preferred_element_type=jnp.float32)
        if pair > 0:
            key_terms += acc_ref[:, :head_dim]
            value_terms += acc_ref[:, head_dim:]
        if pair < pairs - 1:
            acc_ref[:, :head_dim] = key_terms
            acc_ref[:, head_dim:] = value_terms
        else:
            key_terms = key_terms * scale
            near_out_ref[:, :head_dim] = key_terms[:half_rows]
            near_out_ref[:, head_dim:] = value_terms[:half_rows]
            far_out_ref[:, :head_dim] = key_terms[half_rows:].astype(far_out_ref.dtype)
            far_out_ref[:, head_dim:] = value_terms[half_rows:].astype(far_out_ref.dtype)
        query_t = jnp.dot(kt_ref[...], score_grad, preferred_element_type=jnp.float32) * scale
        for half in range(2):
            lo = (2 * pair + half) * head_dim
            dq_held[:, lo : lo + head_dim] = query_t[
                :, half * local_rows : (half + 1) * local_rows
            ].T.astype(dq_held.dtype)
        cols = pl.ds(2 * pair * head_dim, 2 * head_dim)
        copy = pltpu.make_async_copy(
            dq_held.at[:, cols], dq_ref.at[tick, 0, :, cols], dq_sem.at[pair]
        )
        copy.start()
        return copy

    copies = []
    held = front(0)
    for pair in range(pairs):
        following = front(pair + 1) if pair + 1 < pairs else None
        copies.append(back(pair, *held))
        held = following
    for copy in copies:
        copy.wait()


def attend_back(tick, group_order, queries, q_stack, g_stack, kv_arrays, query_grads):
    local_rows, model = queries.shape[2:]
    width = kv_arrays[0].shape[1]
    key_rows = sum(array.shape[0] for array in kv_arrays)
    head_dim = width // 2
    pairs = model // head_dim // 2
    in_vmem = pl.BlockSpec(memory_space=pltpu.VMEM)
    operands = [group_order, q_stack, g_stack, *kv_arrays]
    in_specs = [pl.BlockSpec(memory_space=pltpu.SMEM), *[in_vmem] * (2 + len(kv_arrays))]
    aliases = {}
    if query_grads is not None:
        aliases = {len(operands): 0}
        operands.append(query_grads)
        in_specs.append(pl.BlockSpec(memory_space=pl.ANY))
    tile = (pairs, key_rows, 2 * local_rows)

    def kernel(*refs):
        tick_kernel(tick, len(kv_arrays), len(aliases), *refs)

    return pl.pallas_call(
        kernel,
        out_shape=(
            jax.ShapeDtypeStruct(queries.shape, jnp.bfloat16),
            jax.ShapeDtypeStruct((key_rows // 2, width), jnp.float32),
            jax.ShapeDtypeStruct((key_rows // 2, width), jnp.bfloat16),
        ),
        in_specs=in_specs,
        out_specs=(pl.BlockSpec(memory_space=pl.ANY), in_vmem, in_vmem),
        scratch_shapes=[
            pltpu.VMEM(tile, jnp.float32),
            pltpu.VMEM(tile, jnp.float32),
            pltpu.VMEM(tile, jnp.bfloat16),
            pltpu.VMEM(tile, jnp.bfloat16),
            pltpu.VMEM((key_rows, width), jnp.float32),
            pltpu.VMEM((head_dim, key_rows), jnp.bfloat16),
            pltpu.VMEM((local_rows, model), jnp.bfloat16),
            pltpu.SemaphoreType.DMA((pairs,)),
        ],
        input_output_aliases=aliases,
        compiler_params=pltpu.CompilerParams(vmem_limit_bytes=44 * 2**20),
        cost_estimate=pl.CostEstimate(
            flops=40 * model * key_rows * local_rows,
            bytes_accessed=6 * local_rows * model + 5 * key_rows * width,
            transcendentals=model // head_dim * key_rows * local_rows,
        ),
    )(*operands)


def other_core(block):
    return lax.ppermute(block, "core", [(0, 1), (1, 0)])


def across_chips(block, k):
    return lax.ppermute(block, "z", [(chip, chip ^ k) for chip in range(lax.axis_size("z"))])


def body(
    queries,
    out_grad,
    keys,
    values,
    entering_keys,
    entering_values,
    key_grads_in,
    value_grads_in,
    group_order,
):
    local_rows, head_dim = keys.shape[1:]
    width = 2 * head_dim
    chips = lax.axis_size("z")
    sections = lax.axis_size("section")
    section = lax.axis_index("section")

    own_pair = jnp.concatenate([keys[0], values[0]], axis=1)
    entering_pair = jnp.concatenate([entering_keys, entering_values], axis=1)
    leaving_pair = jnp.where(section == 0, entering_pair, own_pair)

    partners = range(chips - 1, 0, -1)
    near = [across_chips(own_pair, k) for k in partners][::-1]
    own_far = other_core(own_pair)
    next_pair = lax.ppermute(
        leaving_pair, "section", [(i, (i - 1) % sections) for i in range(sections)]
    )
    stacks = stacked_heads(queries, out_grad, head_dim)
    near, next_pair, stacks = lax.optimization_barrier((near, next_pair, stacks))
    far = [own_far] + [other_core(block) for block in near]
    next_far = other_core(next_pair)
    next_near = [across_chips(next_pair, k) for k in partners][::-1]
    query_grads, near_terms, far_terms = attend_back(
        0, group_order, queries, *stacks, [own_pair, *near, *far], None
    )
    query_grads, far_terms, next_near = lax.optimization_barrier(
        (query_grads, far_terms, next_near)
    )
    next_kv = [next_pair, *next_near, next_far, other_core(jnp.concatenate(next_near, axis=0))]

    def chip_sums(near_terms, far_terms):
        sums = near_terms + other_core(far_terms).astype(jnp.float32)
        sums = sums.reshape(chips, local_rows, width)
        return sums[0], [sums[k].astype(jnp.bfloat16) for k in range(1, chips)]

    def reduced(own_sum, leaving):
        for k in partners:
            own_sum = own_sum + across_chips(leaving[k - 1], k).astype(jnp.float32)
        return own_sum

    own_sum, leaving = chip_sums(near_terms, far_terms)
    query_grads, leaving = lax.optimization_barrier((query_grads, leaving))
    first_acc = jnp.concatenate([key_grads_in[0], value_grads_in[0]], axis=1) + reduced(
        own_sum, leaving
    )
    query_grads, near_terms, far_terms = attend_back(
        1, group_order, queries, *stacks, next_kv, query_grads
    )
    first_acc, far_terms = lax.optimization_barrier((first_acc, far_terms))
    moved_acc = lax.ppermute(first_acc, "section", [(i, i - 1) for i in range(1, sections)])
    second_acc = moved_acc + reduced(*chip_sums(near_terms, far_terms))
    key_grads = jnp.stack([first_acc[:, :head_dim], second_acc[:, :head_dim]], axis=0)[:, None]
    value_grads = jnp.stack([first_acc[:, head_dim:], second_acc[:, head_dim:]], axis=0)[:, None]
    return (query_grads, key_grads, value_grads)


def solution(mesh):
    sections, ctx_count = mesh.shape["section"], mesh.shape["ctx"]
    chip_mesh = jax.sharding.Mesh(
        mesh.devices.reshape(sections, ctx_count // 2, 2), ("section", "z", "core")
    )
    tokens = ("z", "core")
    return jax.shard_map(
        body,
        mesh=chip_mesh,
        in_specs=(
            P(None, "section", tokens, None),
            P(None, "section", tokens, None),
            P("section", tokens, None),
            P("section", tokens, None),
            P(tokens, None),
            P(tokens, None),
            P("section", tokens, None),
            P("section", tokens, None),
            P(),
        ),
        out_specs=(
            P(None, "section", tokens, None),
            P(None, "section", tokens, None),
            P(None, "section", tokens, None),
        ),
        check_vma=False,
    )
```

```python
import math

import jax
import jax.numpy as jnp
from jax import lax
from jax.experimental import pallas as pl
from jax.experimental.pallas import tpu as pltpu
from jax.sharding import PartitionSpec as P

MASK_FILL = -1e30
CONTRACT_LAST = (((1,), (1,)), ((), ()))


def stack_kernel(q_ref, g_ref, q_out_ref, g_out_ref):
    ticks, _, local_rows, model = q_ref.shape
    head_dim = q_out_ref.shape[1]
    heads = model // head_dim
    for tick in range(ticks):
        for head in range(heads):
            rows = pl.ds((tick * heads + head) * local_rows, local_rows)
            cols = pl.ds(head * head_dim, head_dim)
            q_out_ref[rows, :] = q_ref[tick, 0, :, cols]
            g_out_ref[rows, :] = g_ref[tick, 0, :, cols]


def stacked_heads(queries, out_grad, head_dim):
    rows = queries.size // head_dim
    in_vmem = pl.BlockSpec(memory_space=pltpu.VMEM)
    return pl.pallas_call(
        stack_kernel,
        out_shape=(jax.ShapeDtypeStruct((rows, head_dim), queries.dtype),) * 2,
        in_specs=[in_vmem, in_vmem],
        out_specs=(in_vmem, in_vmem),
        compiler_params=pltpu.CompilerParams(vmem_limit_bytes=8 * 2**20),
        cost_estimate=pl.CostEstimate(
            flops=queries.size, bytes_accessed=8 * queries.size, transcendentals=0
        ),
    )(queries, out_grad)


def tick_kernel(tick, arrays, aliased, *refs):
    order_ref, q_ref, g_ref = refs[:3]
    outs = refs[3 + arrays + aliased :]
    dq_ref, near_out_ref, far_out_ref = outs[:3]
    e_ref, dp_ref, p_ref, ds_ref, acc_ref, kt_ref, dq_held, dq_sem = outs[3:]
    local_rows, model = dq_held.shape
    head_dim = near_out_ref.shape[1] // 2
    kv_refs = [
        ref.at[pl.ds(row, local_rows)]
        for ref in refs[3 : 3 + arrays]
        for row in range(0, ref.shape[0], local_rows)
    ]
    blocks = len(kv_refs)
    heads = model // head_dim
    pairs = heads // 2
    width = 2 * local_rows
    chips = blocks // 2
    scale = 1.0 / math.sqrt(head_dim)
    exp_scale = scale * math.log2(math.e)

    core = lax.axis_index("core")
    chip = lax.axis_index("z")
    own_group = order_ref[2 * chip + core]

    half = chips // 2 - 1
    mine = [1 + core * half + j for j in range(half)]
    partners = [1 + (1 - core) * half + j for j in range(half)]
    places = [(0, True), (0, False), (chips - 1, True)]
    places += [(k, same) for k in mine for same in (True, False)]
    places += [(chips - 1, False)]
    places += [(k, same) for k in partners for same in (False, True)]

    def allowed(slot):
        k, same = places[slot]
        source = jnp.bitwise_xor(chip, k)
        parity = core if same else 1 - core
        return order_ref[2 * source + parity] < own_group

    for slot in range(blocks):
        kt_ref[:, slot * local_rows : (slot + 1) * local_rows] = kv_refs[slot][:, :head_dim].T

    def pair_of(ref, pair):
        return ref[pl.ds((tick * pairs + pair) * width, width), :]

    def rows_of(slot):
        return slice(slot * local_rows, (slot + 1) * local_rows)

    def front(pair):
        q_pair = pair_of(q_ref, pair)
        g_pair = pair_of(g_ref, pair)
        peaks, totals, weights = [], [], []
        for slot in range(blocks):
            scores = lax.dot_general(
                kv_refs[slot][:, :head_dim],
                q_pair,
                CONTRACT_LAST,
                preferred_element_type=jnp.float32,
            )
            if slot == 0:
                key_row = lax.broadcasted_iota(jnp.int32, (local_rows, width), 0)
                query_row = lax.rem(
                    lax.broadcasted_iota(jnp.int32, (local_rows, width), 1), local_rows
                )
                scores = jnp.where(key_row <= query_row, scores, MASK_FILL)
            peak = jnp.max(scores, axis=0, keepdims=True) * exp_scale
            expo = jnp.exp2(scores * exp_scale - peak)
            prob_grads = lax.dot_general(
                kv_refs[slot][:, head_dim:],
                g_pair,
                CONTRACT_LAST,
                preferred_element_type=jnp.float32,
            )
            e_ref[pair, rows_of(slot)] = expo
            dp_ref[pair, rows_of(slot)] = prob_grads
            peaks.append(peak if slot == 0 else jnp.where(allowed(slot), peak, MASK_FILL))
            totals.append(jnp.sum(expo, axis=0, keepdims=True))
            weights.append(jnp.sum(expo * prob_grads, axis=0, keepdims=True))
        biggest = peaks[0]
        for peak in peaks[1:]:
            biggest = jnp.maximum(biggest, peak)
        factors = [jnp.exp2(peak - biggest) for peak in peaks]
        total = sum(part * factor for part, factor in zip(totals, factors))
        weighted = sum(part * factor for part, factor in zip(weights, factors))
        inverse = 1.0 / total
        return [factor * inverse for factor in factors], weighted * inverse

    def back(pair, factors, delta):
        q_pair = pair_of(q_ref, pair)
        g_pair = pair_of(g_ref, pair)
        for slot in range(blocks):
            probs = e_ref[pair, rows_of(slot)] * factors[slot]
            p_ref[pair, rows_of(slot)] = probs.astype(jnp.bfloat16)
            ds_ref[pair, rows_of(slot)] = (
                probs * (dp_ref[pair, rows_of(slot)] - delta)
            ).astype(jnp.bfloat16)
        score_grad = ds_ref[pair]
        key_terms = jnp.dot(score_grad, q_pair, preferred_element_type=jnp.float32)
        value_terms = jnp.dot(p_ref[pair], g_pair, preferred_element_type=jnp.float32)
        if pair > 0:
            key_terms += acc_ref[:, :head_dim]
            value_terms += acc_ref[:, head_dim:]
        if pair < pairs - 1:
            acc_ref[:, :head_dim] = key_terms
            acc_ref[:, head_dim:] = value_terms
        else:
            for slot, (k, same) in enumerate(places):
                out = near_out_ref if same else far_out_ref
                rows = pl.ds(pl.multiple_of(k * local_rows, local_rows), local_rows)
                out[rows, :head_dim] = (key_terms[rows_of(slot)] * scale).astype(out.dtype)
                out[rows, head_dim:] = value_terms[rows_of(slot)].astype(out.dtype)
        query_t = jnp.dot(kt_ref[...], score_grad, preferred_element_type=jnp.float32) * scale
        for half in range(2):
            lo = (2 * pair + half) * head_dim
            dq_held[:, lo : lo + head_dim] = query_t[
                :, half * local_rows : (half + 1) * local_rows
            ].T.astype(dq_held.dtype)
        cols = pl.ds(2 * pair * head_dim, 2 * head_dim)
        copy = pltpu.make_async_copy(
            dq_held.at[:, cols], dq_ref.at[tick, 0, :, cols], dq_sem.at[pair]
        )
        copy.start()
        return copy

    copies = []
    held = front(0)
    for pair in range(pairs):
        following = front(pair + 1) if pair + 1 < pairs else None
        copies.append(back(pair, *held))
        held = following
    for copy in copies:
        copy.wait()


def attend_back(tick, group_order, queries, q_stack, g_stack, kv_arrays, query_grads):
    local_rows, model = queries.shape[2:]
    width = kv_arrays[0].shape[1]
    key_rows = sum(array.shape[0] for array in kv_arrays)
    head_dim = width // 2
    pairs = model // head_dim // 2
    in_vmem = pl.BlockSpec(memory_space=pltpu.VMEM)
    operands = [group_order, q_stack, g_stack, *kv_arrays]
    in_specs = [pl.BlockSpec(memory_space=pltpu.SMEM), *[in_vmem] * (2 + len(kv_arrays))]
    aliases = {}
    if query_grads is not None:
        aliases = {len(operands): 0}
        operands.append(query_grads)
        in_specs.append(pl.BlockSpec(memory_space=pl.ANY))
    tile = (pairs, key_rows, 2 * local_rows)

    def kernel(*refs):
        tick_kernel(tick, len(kv_arrays), len(aliases), *refs)

    return pl.pallas_call(
        kernel,
        out_shape=(
            jax.ShapeDtypeStruct(queries.shape, jnp.bfloat16),
            jax.ShapeDtypeStruct((key_rows // 2, width), jnp.float32),
            jax.ShapeDtypeStruct((key_rows // 2, width), jnp.bfloat16),
        ),
        in_specs=in_specs,
        out_specs=(pl.BlockSpec(memory_space=pl.ANY), in_vmem, in_vmem),
        scratch_shapes=[
            pltpu.VMEM(tile, jnp.float32),
            pltpu.VMEM(tile, jnp.float32),
            pltpu.VMEM(tile, jnp.bfloat16),
            pltpu.VMEM(tile, jnp.bfloat16),
            pltpu.VMEM((key_rows, width), jnp.float32),
            pltpu.VMEM((head_dim, key_rows), jnp.bfloat16),
            pltpu.VMEM((local_rows, model), jnp.bfloat16),
            pltpu.SemaphoreType.DMA((pairs,)),
        ],
        input_output_aliases=aliases,
        compiler_params=pltpu.CompilerParams(vmem_limit_bytes=44 * 2**20),
        cost_estimate=pl.CostEstimate(
            flops=40 * model * key_rows * local_rows,
            bytes_accessed=6 * local_rows * model + 5 * key_rows * width,
            transcendentals=model // head_dim * key_rows * local_rows,
        ),
    )(*operands)


def other_core(block):
    return lax.ppermute(block, "core", [(0, 1), (1, 0)])


def across_chips(block, k):
    return lax.ppermute(block, "z", [(chip, chip ^ k) for chip in range(lax.axis_size("z"))])


def across_pairs(blocks, j):
    chips = lax.axis_size("z")
    route = [
        (2 * chip + core, 2 * (chip ^ (1 + core * (chips // 2 - 1) + j)) + core)
        for chip in range(chips)
        for core in range(2)
    ]
    return lax.ppermute(blocks, ("z", "core"), route)


def gathered(own, own_far):
    chips = lax.axis_size("z")
    shared = across_chips(own, chips - 1)
    both = jnp.concatenate([own, own_far], axis=0)
    return [shared, *[across_pairs(both, j) for j in range(chips // 2 - 1)]]


def body(
    queries,
    out_grad,
    keys,
    values,
    entering_keys,
    entering_values,
    key_grads_in,
    value_grads_in,
    group_order,
):
    local_rows, head_dim = keys.shape[1:]
    width = 2 * head_dim
    chips = lax.axis_size("z")
    sections = lax.axis_size("section")
    section = lax.axis_index("section")

    own_pair = jnp.concatenate([keys[0], values[0]], axis=1)
    entering_pair = jnp.concatenate([entering_keys, entering_values], axis=1)
    leaving_pair = jnp.where(section == 0, entering_pair, own_pair)

    own_far = other_core(own_pair)
    shared, *pairs = gathered(own_pair, own_far)
    next_pair = lax.ppermute(
        leaving_pair, "section", [(i, (i - 1) % sections) for i in range(sections)]
    )
    stacks = stacked_heads(queries, out_grad, head_dim)
    pairs, next_pair, stacks = lax.optimization_barrier((pairs, next_pair, stacks))
    next_far = other_core(next_pair)
    partner_blocks = [other_core(block) for block in (shared, *pairs)]
    next_blocks = gathered(next_pair, next_far)
    query_grads, near_terms, far_terms = attend_back(
        0,
        group_order,
        queries,
        *stacks,
        [own_pair, own_far, shared, *pairs, *partner_blocks],
        None,
    )
    query_grads, far_terms, next_blocks = lax.optimization_barrier(
        (query_grads, far_terms, next_blocks)
    )
    partner_blocks = other_core(jnp.concatenate(next_blocks, axis=0))
    next_kv = [next_pair, next_far, *next_blocks, partner_blocks]

    def chip_sums(near_terms, far_terms):
        sums = near_terms + other_core(far_terms).astype(jnp.float32)
        sums = sums.reshape(chips, local_rows, width)
        return sums[0], [sums[k].astype(jnp.bfloat16) for k in range(1, chips)]

    def reduced(own_sum, leaving):
        for k in range(chips - 1, 0, -1):
            own_sum = own_sum + across_chips(leaving[k - 1], k).astype(jnp.float32)
        return own_sum

    own_sum, leaving = chip_sums(near_terms, far_terms)
    query_grads, leaving = lax.optimization_barrier((query_grads, leaving))
    first_acc = jnp.concatenate([key_grads_in[0], value_grads_in[0]], axis=1) + reduced(
        own_sum, leaving
    )
    query_grads, near_terms, far_terms = attend_back(
        1, group_order, queries, *stacks, next_kv, query_grads
    )
    first_acc, far_terms = lax.optimization_barrier((first_acc, far_terms))
    odd_acc = lax.ppermute(first_acc, "section", [(i, i - 1) for i in range(1, sections, 2)])
    own_sum, leaving = chip_sums(near_terms, far_terms)
    late_acc, leaving = lax.optimization_barrier((first_acc.astype(jnp.bfloat16), leaving))
    second_acc = reduced(own_sum + odd_acc, leaving)
    even_acc = lax.ppermute(late_acc, "section", [(i, i - 1) for i in range(2, sections, 2)])
    second_acc = second_acc + even_acc.astype(jnp.float32)
    key_grads = jnp.stack([first_acc[:, :head_dim], second_acc[:, :head_dim]], axis=0)[:, None]
    value_grads = jnp.stack([first_acc[:, head_dim:], second_acc[:, head_dim:]], axis=0)[:, None]
    return (query_grads, key_grads, value_grads)


def solution(mesh):
    sections, ctx_count = mesh.shape["section"], mesh.shape["ctx"]
    chip_mesh = jax.sharding.Mesh(
        mesh.devices.reshape(sections, ctx_count // 2, 2), ("section", "z", "core")
    )
    tokens = ("z", "core")
    return jax.shard_map(
        body,
        mesh=chip_mesh,
        in_specs=(
            P(None, "section", tokens, None),
            P(None, "section", tokens, None),
            P("section", tokens, None),
            P("section", tokens, None),
            P(tokens, None),
            P(tokens, None),
            P("section", tokens, None),
            P("section", tokens, None),
            P(),
        ),
        out_specs=(
            P(None, "section", tokens, None),
            P(None, "section", tokens, None),
            P(None, "section", tokens, None),
        ),
        check_vma=False,
    )
```

```python
import math

import jax
import jax.numpy as jnp
from jax import lax
from jax.experimental import pallas as pl
from jax.experimental.pallas import tpu as pltpu
from jax.sharding import PartitionSpec as P

MASK_FILL = -1e30
CONTRACT_LAST = (((1,), (1,)), ((), ()))


def stack_kernel(q_ref, g_ref, q_out_ref, g_out_ref):
    ticks, _, local_rows, model = q_ref.shape
    head_dim = q_out_ref.shape[1]
    heads = model // head_dim
    for tick in range(ticks):
        for head in range(heads):
            rows = pl.ds((tick * heads + head) * local_rows, local_rows)
            cols = pl.ds(head * head_dim, head_dim)
            q_out_ref[rows, :] = q_ref[tick, 0, :, cols]
            g_out_ref[rows, :] = g_ref[tick, 0, :, cols]


def stacked_heads(queries, out_grad, head_dim):
    rows = queries.size // head_dim
    in_vmem = pl.BlockSpec(memory_space=pltpu.VMEM)
    return pl.pallas_call(
        stack_kernel,
        out_shape=(jax.ShapeDtypeStruct((rows, head_dim), queries.dtype),) * 2,
        in_specs=[in_vmem, in_vmem],
        out_specs=(in_vmem, in_vmem),
        compiler_params=pltpu.CompilerParams(vmem_limit_bytes=8 * 2**20),
        cost_estimate=pl.CostEstimate(
            flops=queries.size, bytes_accessed=8 * queries.size, transcendentals=0
        ),
    )(queries, out_grad)


def tick_kernel(tick, arrays, aliased, *refs):
    order_ref, q_ref, g_ref = refs[:3]
    outs = refs[3 + arrays + aliased :]
    dq_ref, near_out_ref, far_out_ref = outs[:3]
    e_ref, dp_ref, p_ref, ds_ref, acc_ref, kt_ref, dq_held, dq_sem = outs[3:]
    local_rows, model = dq_held.shape
    head_dim = near_out_ref.shape[1] // 2
    half_rows = near_out_ref.shape[0]
    kv_refs = [
        ref.at[pl.ds(row, local_rows)]
        for ref in refs[3 : 3 + arrays]
        for row in range(0, ref.shape[0], local_rows)
    ]
    blocks = len(kv_refs)
    heads = model // head_dim
    pairs = heads // 2
    width = 2 * local_rows
    chips = blocks // 2
    scale = 1.0 / math.sqrt(head_dim)
    exp_scale = scale * math.log2(math.e)

    core = lax.axis_index("core")
    chip = lax.axis_index("z")
    own_group = order_ref[2 * chip + core]

    def allowed(slot):
        source = jnp.bitwise_xor(chip, slot % chips)
        parity = core if slot < chips else 1 - core
        return order_ref[2 * source + parity] < own_group

    for slot in range(blocks):
        kt_ref[:, slot * local_rows : (slot + 1) * local_rows] = kv_refs[slot][:, :head_dim].T

    def pair_of(ref, pair):
        return ref[pl.ds((tick * pairs + pair) * width, width), :]

    def rows_of(slot):
        return slice(slot * local_rows, (slot + 1) * local_rows)

    def front(pair):
        q_pair = pair_of(q_ref, pair)
        g_pair = pair_of(g_ref, pair)
        peaks, totals, weights = [], [], []
        for slot in range(blocks):
            scores = lax.dot_general(
                kv_refs[slot][:, :head_dim],
                q_pair,
                CONTRACT_LAST,
                preferred_element_type=jnp.float32,
            )
            if slot == 0:
                key_row = lax.broadcasted_iota(jnp.int32, (local_rows, width), 0)
                query_row = lax.rem(
                    lax.broadcasted_iota(jnp.int32, (local_rows, width), 1), local_rows
                )
                scores = jnp.where(key_row <= query_row, scores, MASK_FILL)
            peak = jnp.max(scores, axis=0, keepdims=True) * exp_scale
            expo = jnp.exp2(scores * exp_scale - peak)
            prob_grads = lax.dot_general(
                kv_refs[slot][:, head_dim:],
                g_pair,
                CONTRACT_LAST,
                preferred_element_type=jnp.float32,
            )
            e_ref[pair, rows_of(slot)] = expo
            dp_ref[pair, rows_of(slot)] = prob_grads
            peaks.append(peak if slot == 0 else jnp.where(allowed(slot), peak, MASK_FILL))
            totals.append(jnp.sum(expo, axis=0, keepdims=True))
            weights.append(jnp.sum(expo * prob_grads, axis=0, keepdims=True))
        biggest = peaks[0]
        for peak in peaks[1:]:
            biggest = jnp.maximum(biggest, peak)
        factors = [jnp.exp2(peak - biggest) for peak in peaks]
        total = sum(part * factor for part, factor in zip(totals, factors))
        weighted = sum(part * factor for part, factor in zip(weights, factors))
        inverse = 1.0 / total
        return [factor * inverse for factor in factors], weighted * inverse

    def back(pair, factors, delta):
        q_pair = pair_of(q_ref, pair)
        g_pair = pair_of(g_ref, pair)
        for slot in range(blocks):
            probs = e_ref[pair, rows_of(slot)] * factors[slot]
            p_ref[pair, rows_of(slot)] = probs.astype(jnp.bfloat16)
            ds_ref[pair, rows_of(slot)] = (
                probs * (dp_ref[pair, rows_of(slot)] - delta)
            ).astype(jnp.bfloat16)
        score_grad = ds_ref[pair]
        key_terms = jnp.dot(score_grad, q_pair, preferred_element_type=jnp.float32)
        value_terms = jnp.dot(p_ref[pair], g_pair, preferred_element_type=jnp.float32)
        if pair > 0:
            key_terms += acc_ref[:, :head_dim]
            value_terms += acc_ref[:, head_dim:]
        if pair < pairs - 1:
            acc_ref[:, :head_dim] = key_terms
            acc_ref[:, head_dim:] = value_terms
        else:
            key_terms = key_terms * scale
            near_out_ref[:, :head_dim] = key_terms[:half_rows]
            near_out_ref[:, head_dim:] = value_terms[:half_rows]
            far_out_ref[:, :head_dim] = key_terms[half_rows:].astype(far_out_ref.dtype)
            far_out_ref[:, head_dim:] = value_terms[half_rows:].astype(far_out_ref.dtype)
        query_t = jnp.dot(kt_ref[...], score_grad, preferred_element_type=jnp.float32) * scale
        for half in range(2):
            lo = (2 * pair + half) * head_dim
            dq_held[:, lo : lo + head_dim] = query_t[
                :, half * local_rows : (half + 1) * local_rows
            ].T.astype(dq_held.dtype)
        cols = pl.ds(2 * pair * head_dim, 2 * head_dim)
        copy = pltpu.make_async_copy(
            dq_held.at[:, cols], dq_ref.at[tick, 0, :, cols], dq_sem.at[pair]
        )
        copy.start()
        return copy

    copies = []
    held = front(0)
    for pair in range(pairs):
        following = front(pair + 1) if pair + 1 < pairs else None
        copies.append(back(pair, *held))
        held = following
    for copy in copies:
        copy.wait()


def attend_back(tick, group_order, queries, q_stack, g_stack, kv_arrays, query_grads):
    local_rows, model = queries.shape[2:]
    width = kv_arrays[0].shape[1]
    key_rows = sum(array.shape[0] for array in kv_arrays)
    head_dim = width // 2
    pairs = model // head_dim // 2
    in_vmem = pl.BlockSpec(memory_space=pltpu.VMEM)
    operands = [group_order, q_stack, g_stack, *kv_arrays]
    in_specs = [pl.BlockSpec(memory_space=pltpu.SMEM), *[in_vmem] * (2 + len(kv_arrays))]
    aliases = {}
    if query_grads is not None:
        aliases = {len(operands): 0}
        operands.append(query_grads)
        in_specs.append(pl.BlockSpec(memory_space=pl.ANY))
    tile = (pairs, key_rows, 2 * local_rows)

    def kernel(*refs):
        tick_kernel(tick, len(kv_arrays), len(aliases), *refs)

    return pl.pallas_call(
        kernel,
        out_shape=(
            jax.ShapeDtypeStruct(queries.shape, jnp.bfloat16),
            jax.ShapeDtypeStruct((key_rows // 2, width), jnp.float32),
            jax.ShapeDtypeStruct((key_rows // 2, width), jnp.bfloat16),
        ),
        in_specs=in_specs,
        out_specs=(pl.BlockSpec(memory_space=pl.ANY), in_vmem, in_vmem),
        scratch_shapes=[
            pltpu.VMEM(tile, jnp.float32),
            pltpu.VMEM(tile, jnp.float32),
            pltpu.VMEM(tile, jnp.bfloat16),
            pltpu.VMEM(tile, jnp.bfloat16),
            pltpu.VMEM((key_rows, width), jnp.float32),
            pltpu.VMEM((head_dim, key_rows), jnp.bfloat16),
            pltpu.VMEM((local_rows, model), jnp.bfloat16),
            pltpu.SemaphoreType.DMA((pairs,)),
        ],
        input_output_aliases=aliases,
        compiler_params=pltpu.CompilerParams(vmem_limit_bytes=44 * 2**20),
        cost_estimate=pl.CostEstimate(
            flops=40 * model * key_rows * local_rows,
            bytes_accessed=6 * local_rows * model + 5 * key_rows * width,
            transcendentals=model // head_dim * key_rows * local_rows,
        ),
    )(*operands)


def other_core(block):
    return lax.ppermute(block, "core", [(0, 1), (1, 0)])


def across_chips(block, k):
    return lax.ppermute(block, "z", [(chip, chip ^ k) for chip in range(lax.axis_size("z"))])


def section_swap(block, first):
    sections = lax.axis_size("section")
    route = []
    for low in range(first, sections, 2):
        high = (low + 1) % sections
        route += [(low, high), (high, low)]
    return lax.ppermute(block, "section", route)


def body(
    queries,
    out_grad,
    keys,
    values,
    entering_keys,
    entering_values,
    key_grads_in,
    value_grads_in,
    group_order,
):
    local_rows, head_dim = keys.shape[1:]
    width = 2 * head_dim
    chips = lax.axis_size("z")
    sections = lax.axis_size("section")
    section = lax.axis_index("section")

    own_pair = jnp.concatenate([keys[0], values[0]], axis=1)
    entering_pair = jnp.concatenate([entering_keys, entering_values], axis=1)
    leaving_pair = jnp.where(section == 0, entering_pair, own_pair)

    partners = range(chips - 1, 0, -1)
    near = [across_chips(own_pair, k) for k in partners][::-1]
    own_far = other_core(own_pair)
    next_pair = lax.ppermute(
        leaving_pair, "section", [(i, (i - 1) % sections) for i in range(sections)]
    )
    stacks = stacked_heads(queries, out_grad, head_dim)
    near, next_pair, stacks = lax.optimization_barrier((near, next_pair, stacks))
    far = [own_far] + [other_core(block) for block in near]
    next_far = other_core(next_pair)
    next_near = [across_chips(next_pair, k) for k in partners][::-1]
    query_grads, near_terms, far_terms = attend_back(
        0, group_order, queries, *stacks, [own_pair, *near, *far], None
    )
    query_grads, far_terms, next_near = lax.optimization_barrier(
        (query_grads, far_terms, next_near)
    )
    next_kv = [next_pair, *next_near, next_far, other_core(jnp.concatenate(next_near, axis=0))]

    def chip_sums(near_terms, far_terms):
        sums = near_terms + other_core(far_terms).astype(jnp.float32)
        sums = sums.reshape(chips, local_rows, width)
        return sums[0], [sums[k].astype(jnp.bfloat16) for k in range(1, chips)]

    def reduced(own_sum, leaving):
        for k in partners:
            own_sum = own_sum + across_chips(leaving[k - 1], k).astype(jnp.float32)
        return own_sum

    own_sum, leaving = chip_sums(near_terms, far_terms)
    query_grads, leaving = lax.optimization_barrier((query_grads, leaving))
    first_acc = jnp.concatenate([key_grads_in[0], value_grads_in[0]], axis=1) + reduced(
        own_sum, leaving
    )
    query_grads, near_terms, far_terms = attend_back(
        1, group_order, queries, *stacks, next_kv, query_grads
    )
    first_acc, far_terms = lax.optimization_barrier((first_acc, far_terms))
    early_acc = section_swap(first_acc, 0)
    own_sum, leaving = chip_sums(near_terms, far_terms)
    late_acc, leaving = lax.optimization_barrier((first_acc.astype(jnp.bfloat16), leaving))
    second_acc = reduced(own_sum, leaving)
    late_acc = section_swap(late_acc, 1).astype(jnp.float32)
    moved_acc = jnp.where(section % 2 == 0, early_acc, late_acc)
    second_acc = second_acc + jnp.where(section == sections - 1, 0.0, moved_acc)
    key_grads = jnp.stack([first_acc[:, :head_dim], second_acc[:, :head_dim]], axis=0)[:, None]
    value_grads = jnp.stack([first_acc[:, head_dim:], second_acc[:, head_dim:]], axis=0)[:, None]
    return (query_grads, key_grads, value_grads)


def solution(mesh):
    sections, ctx_count = mesh.shape["section"], mesh.shape["ctx"]
    chip_mesh = jax.sharding.Mesh(
        mesh.devices.reshape(sections, ctx_count // 2, 2), ("section", "z", "core")
    )
    tokens = ("z", "core")
    return jax.shard_map(
        body,
        mesh=chip_mesh,
        in_specs=(
            P(None, "section", tokens, None),
            P(None, "section", tokens, None),
            P("section", tokens, None),
            P("section", tokens, None),
            P(tokens, None),
            P(tokens, None),
            P("section", tokens, None),
            P("section", tokens, None),
            P(),
        ),
        out_specs=(
            P(None, "section", tokens, None),
            P(None, "section", tokens, None),
            P(None, "section", tokens, None),
        ),
        check_vma=False,
    )
```

```python
import math

import jax
import jax.numpy as jnp
from jax import lax
from jax.experimental import pallas as pl
from jax.experimental.pallas import tpu as pltpu
from jax.sharding import PartitionSpec as P

MASK_FILL = -1e30
CONTRACT_LAST = (((1,), (1,)), ((), ()))


def stack_kernel(q_ref, g_ref, q_out_ref, g_out_ref):
    ticks, _, local_rows, model = q_ref.shape
    head_dim = q_out_ref.shape[1]
    heads = model // head_dim
    for tick in range(ticks):
        for head in range(heads):
            rows = pl.ds((tick * heads + head) * local_rows, local_rows)
            cols = pl.ds(head * head_dim, head_dim)
            q_out_ref[rows, :] = q_ref[tick, 0, :, cols]
            g_out_ref[rows, :] = g_ref[tick, 0, :, cols]


def stacked_heads(queries, out_grad, head_dim):
    rows = queries.size // head_dim
    in_vmem = pl.BlockSpec(memory_space=pltpu.VMEM)
    return pl.pallas_call(
        stack_kernel,
        out_shape=(jax.ShapeDtypeStruct((rows, head_dim), queries.dtype),) * 2,
        in_specs=[in_vmem, in_vmem],
        out_specs=(in_vmem, in_vmem),
        compiler_params=pltpu.CompilerParams(vmem_limit_bytes=8 * 2**20),
        cost_estimate=pl.CostEstimate(
            flops=queries.size, bytes_accessed=8 * queries.size, transcendentals=0
        ),
    )(queries, out_grad)


def tick_kernel(tick, arrays, aliased, *refs):
    order_ref, q_ref, g_ref = refs[:3]
    outs = refs[3 + arrays + aliased :]
    dq_ref, near_out_ref, far_out_ref = outs[:3]
    e_ref, dp_ref, p_ref, ds_ref, acc_ref, kv_ref, kt_ref, dq_held, dq_sem = outs[3:]
    local_rows, model = dq_held.shape
    head_dim = near_out_ref.shape[1] // 2
    half_rows = near_out_ref.shape[0]
    kv_refs = [
        ref.at[pl.ds(row, local_rows)]
        for ref in refs[3 : 3 + arrays]
        for row in range(0, ref.shape[0], local_rows)
    ]
    blocks = len(kv_refs)
    heads = model // head_dim
    pairs = heads // 2
    width = 2 * local_rows
    chips = blocks // 2
    scale = 1.0 / math.sqrt(head_dim)
    exp_scale = scale * math.log2(math.e)

    core = lax.axis_index("core")
    chip = lax.axis_index("z")
    own_group = order_ref[2 * chip + core]

    def allowed(slot):
        source = jnp.bitwise_xor(chip, slot % chips)
        parity = core if slot < chips else 1 - core
        return order_ref[2 * source + parity] < own_group

    def rows_of(slot):
        return slice(slot * local_rows, (slot + 1) * local_rows)

    for slot in range(blocks):
        block = kv_refs[slot][...]
        kv_ref[rows_of(slot), :] = block
        kt_ref[:, rows_of(slot)] = block[:, :head_dim].T

    def stacked(ref, first, last):
        return ref[pl.ds((tick * pairs + first) * width, (last - first) * width), :]

    def products(pair):
        for out, ref, cols in (
            (e_ref, q_ref, slice(0, head_dim)),
            (dp_ref, g_ref, slice(head_dim, 2 * head_dim)),
        ):
            out[pair] = lax.dot_general(
                kv_ref[:, cols],
                stacked(ref, pair, pair + 1),
                CONTRACT_LAST,
                preferred_element_type=jnp.float32,
            )

    def softmax(pair):
        peaks, totals, weights = [], [], []
        for slot in range(blocks):
            scores = e_ref[pair, rows_of(slot)]
            if slot == 0:
                key_row = lax.broadcasted_iota(jnp.int32, (local_rows, width), 0)
                query_row = lax.rem(
                    lax.broadcasted_iota(jnp.int32, (local_rows, width), 1), local_rows
                )
                scores = jnp.where(key_row <= query_row, scores, MASK_FILL)
            peak = jnp.max(scores, axis=0, keepdims=True) * exp_scale
            expo = jnp.exp2(scores * exp_scale - peak)
            e_ref[pair, rows_of(slot)] = expo
            peaks.append(peak if slot == 0 else jnp.where(allowed(slot), peak, MASK_FILL))
            totals.append(jnp.sum(expo, axis=0, keepdims=True))
            weights.append(jnp.sum(expo * dp_ref[pair, rows_of(slot)], axis=0, keepdims=True))
        biggest = peaks[0]
        for peak in peaks[1:]:
            biggest = jnp.maximum(biggest, peak)
        factors = [jnp.exp2(peak - biggest) for peak in peaks]
        total = sum(part * factor for part, factor in zip(totals, factors))
        weighted = sum(part * factor for part, factor in zip(weights, factors))
        inverse = 1.0 / total
        delta = weighted * inverse
        cols = slice(pair * width, (pair + 1) * width)
        for slot in range(blocks):
            probs = e_ref[pair, rows_of(slot)] * (factors[slot] * inverse)
            p_ref[rows_of(slot), cols] = probs.astype(jnp.bfloat16)
            ds_ref[rows_of(slot), cols] = (
                probs * (dp_ref[pair, rows_of(slot)] - delta)
            ).astype(jnp.bfloat16)

    def query_grad(pair):
        query_t = jnp.dot(
            kt_ref[...],
            ds_ref[:, pair * width : (pair + 1) * width],
            preferred_element_type=jnp.float32,
        )
        for half in range(2):
            lo = (2 * pair + half) * head_dim
            dq_held[:, lo : lo + head_dim] = (
                query_t[:, half * local_rows : (half + 1) * local_rows].T * scale
            ).astype(dq_held.dtype)
        cols = pl.ds(2 * pair * head_dim, 2 * head_dim)
        copy = pltpu.make_async_copy(
            dq_held.at[:, cols], dq_ref.at[tick, 0, :, cols], dq_sem.at[pair]
        )
        copy.start()
        return copy

    def terms(first, last):
        cols = slice(first * width, last * width)
        return tuple(
            jnp.dot(
                held[:, cols], stacked(ref, first, last), preferred_element_type=jnp.float32
            )
            for held, ref in ((ds_ref, q_ref), (p_ref, g_ref))
        )

    copies = []
    products(0)
    for pair in range(pairs):
        if pair + 1 < pairs:
            products(pair + 1)
        if pair and pair + 1 == pairs:
            acc_ref[:, :head_dim], acc_ref[:, head_dim:] = terms(0, pair)
        softmax(pair)
        copies.append(query_grad(pair))
    key_terms, value_terms = terms(pairs - 1, pairs)
    if pairs > 1:
        key_terms += acc_ref[:, :head_dim]
        value_terms += acc_ref[:, head_dim:]
    near_out_ref[:, :head_dim] = key_terms[:half_rows] * scale
    near_out_ref[:, head_dim:] = value_terms[:half_rows]
    far_out_ref[:, :head_dim] = (key_terms[half_rows:] * scale).astype(far_out_ref.dtype)
    far_out_ref[:, head_dim:] = value_terms[half_rows:].astype(far_out_ref.dtype)
    for copy in copies:
        copy.wait()


def attend_back(tick, group_order, queries, q_stack, g_stack, kv_arrays, query_grads):
    local_rows, model = queries.shape[2:]
    width = kv_arrays[0].shape[1]
    key_rows = sum(array.shape[0] for array in kv_arrays)
    head_dim = width // 2
    pairs = model // head_dim // 2
    in_vmem = pl.BlockSpec(memory_space=pltpu.VMEM)
    operands = [group_order, q_stack, g_stack, *kv_arrays]
    in_specs = [pl.BlockSpec(memory_space=pltpu.SMEM), *[in_vmem] * (2 + len(kv_arrays))]
    aliases = {}
    if query_grads is not None:
        aliases = {len(operands): 0}
        operands.append(query_grads)
        in_specs.append(pl.BlockSpec(memory_space=pl.ANY))
    tile = (pairs, key_rows, 2 * local_rows)

    def kernel(*refs):
        tick_kernel(tick, len(kv_arrays), len(aliases), *refs)

    return pl.pallas_call(
        kernel,
        out_shape=(
            jax.ShapeDtypeStruct(queries.shape, jnp.bfloat16),
            jax.ShapeDtypeStruct((key_rows // 2, width), jnp.float32),
            jax.ShapeDtypeStruct((key_rows // 2, width), jnp.bfloat16),
        ),
        in_specs=in_specs,
        out_specs=(pl.BlockSpec(memory_space=pl.ANY), in_vmem, in_vmem),
        scratch_shapes=[
            pltpu.VMEM(tile, jnp.float32),
            pltpu.VMEM(tile, jnp.float32),
            pltpu.VMEM((key_rows, 2 * pairs * local_rows), jnp.bfloat16),
            pltpu.VMEM((key_rows, 2 * pairs * local_rows), jnp.bfloat16),
            pltpu.VMEM((key_rows, width), jnp.float32),
            pltpu.VMEM((key_rows, width), jnp.bfloat16),
            pltpu.VMEM((head_dim, key_rows), jnp.bfloat16),
            pltpu.VMEM((local_rows, model), jnp.bfloat16),
            pltpu.SemaphoreType.DMA((pairs,)),
        ],
        input_output_aliases=aliases,
        compiler_params=pltpu.CompilerParams(vmem_limit_bytes=44 * 2**20),
        cost_estimate=pl.CostEstimate(
            flops=40 * model * key_rows * local_rows,
            bytes_accessed=6 * local_rows * model + 5 * key_rows * width,
            transcendentals=model // head_dim * key_rows * local_rows,
        ),
    )(*operands)


def other_core(block):
    return lax.ppermute(block, "core", [(0, 1), (1, 0)])


def across_chips(block, k):
    return lax.ppermute(block, "z", [(chip, chip ^ k) for chip in range(lax.axis_size("z"))])


def section_swap(block, first):
    sections = lax.axis_size("section")
    route = []
    for low in range(first, sections, 2):
        high = (low + 1) % sections
        route += [(low, high), (high, low)]
    return lax.ppermute(block, "section", route)


def body(
    queries,
    out_grad,
    keys,
    values,
    entering_keys,
    entering_values,
    key_grads_in,
    value_grads_in,
    group_order,
):
    local_rows, head_dim = keys.shape[1:]
    width = 2 * head_dim
    chips = lax.axis_size("z")
    sections = lax.axis_size("section")
    section = lax.axis_index("section")

    own_pair = jnp.concatenate([keys[0], values[0]], axis=1)
    entering_pair = jnp.concatenate([entering_keys, entering_values], axis=1)
    leaving_pair = jnp.where(section == 0, entering_pair, own_pair)

    partners = range(chips - 1, 0, -1)
    near = [across_chips(own_pair, k) for k in partners][::-1]
    own_far = other_core(own_pair)
    next_pair = lax.ppermute(
        leaving_pair, "section", [(i, (i - 1) % sections) for i in range(sections)]
    )
    stacks = stacked_heads(queries, out_grad, head_dim)
    near, next_pair, stacks = lax.optimization_barrier((near, next_pair, stacks))
    far = [own_far] + [other_core(block) for block in near]
    next_far = other_core(next_pair)
    next_near = [across_chips(next_pair, k) for k in partners][::-1]
    query_grads, near_terms, far_terms = attend_back(
        0, group_order, queries, *stacks, [own_pair, *near, *far], None
    )
    query_grads, far_terms, next_near = lax.optimization_barrier(
        (query_grads, far_terms, next_near)
    )
    next_kv = [next_pair, *next_near, next_far, other_core(jnp.concatenate(next_near, axis=0))]

    def chip_sums(near_terms, far_terms):
        sums = near_terms + other_core(far_terms).astype(jnp.float32)
        sums = sums.reshape(chips, local_rows, width)
        return sums[0], [sums[k].astype(jnp.bfloat16) for k in range(1, chips)]

    def reduced(own_sum, leaving):
        for k in partners:
            own_sum = own_sum + across_chips(leaving[k - 1], k).astype(jnp.float32)
        return own_sum

    own_sum, leaving = chip_sums(near_terms, far_terms)
    query_grads, leaving = lax.optimization_barrier((query_grads, leaving))
    first_acc = jnp.concatenate([key_grads_in[0], value_grads_in[0]], axis=1) + reduced(
        own_sum, leaving
    )
    query_grads, near_terms, far_terms = attend_back(
        1, group_order, queries, *stacks, next_kv, query_grads
    )
    first_acc, far_terms = lax.optimization_barrier((first_acc, far_terms))
    early_acc = section_swap(first_acc, 0)
    own_sum, leaving = chip_sums(near_terms, far_terms)
    late_acc, leaving = lax.optimization_barrier((first_acc.astype(jnp.bfloat16), leaving))
    second_acc = reduced(own_sum, leaving)
    late_acc = section_swap(late_acc, 1).astype(jnp.float32)
    moved_acc = jnp.where(section % 2 == 0, early_acc, late_acc)
    second_acc = second_acc + jnp.where(section == sections - 1, 0.0, moved_acc)
    key_grads = jnp.stack([first_acc[:, :head_dim], second_acc[:, :head_dim]], axis=0)[:, None]
    value_grads = jnp.stack([first_acc[:, head_dim:], second_acc[:, head_dim:]], axis=0)[:, None]
    return (query_grads, key_grads, value_grads)


def solution(mesh):
    sections, ctx_count = mesh.shape["section"], mesh.shape["ctx"]
    chip_mesh = jax.sharding.Mesh(
        mesh.devices.reshape(sections, ctx_count // 2, 2), ("section", "z", "core")
    )
    tokens = ("z", "core")
    return jax.shard_map(
        body,
        mesh=chip_mesh,
        in_specs=(
            P(None, "section", tokens, None),
            P(None, "section", tokens, None),
            P("section", tokens, None),
            P("section", tokens, None),
            P(tokens, None),
            P(tokens, None),
            P("section", tokens, None),
            P("section", tokens, None),
            P(),
        ),
        out_specs=(
            P(None, "section", tokens, None),
            P(None, "section", tokens, None),
            P(None, "section", tokens, None),
        ),
        check_vma=False,
    )
```

```python
import math

import jax
import jax.numpy as jnp
from jax import lax
from jax.experimental import pallas as pl
from jax.experimental.pallas import tpu as pltpu
from jax.sharding import PartitionSpec as P

MASK_FILL = -1e30
CONTRACT_LAST = (((1,), (1,)), ((), ()))


def stack_kernel(q_ref, g_ref, q_out_ref, g_out_ref):
    ticks, _, local_rows, model = q_ref.shape
    head_dim = q_out_ref.shape[1]
    heads = model // head_dim
    for tick in range(ticks):
        for head in range(heads):
            rows = pl.ds((tick * heads + head) * local_rows, local_rows)
            cols = pl.ds(head * head_dim, head_dim)
            q_out_ref[rows, :] = q_ref[tick, 0, :, cols]
            g_out_ref[rows, :] = g_ref[tick, 0, :, cols]


def stacked_heads(queries, out_grad, head_dim):
    rows = queries.size // head_dim
    in_vmem = pl.BlockSpec(memory_space=pltpu.VMEM)
    return pl.pallas_call(
        stack_kernel,
        out_shape=(jax.ShapeDtypeStruct((rows, head_dim), queries.dtype),) * 2,
        in_specs=[in_vmem, in_vmem],
        out_specs=(in_vmem, in_vmem),
        compiler_params=pltpu.CompilerParams(vmem_limit_bytes=8 * 2**20),
        cost_estimate=pl.CostEstimate(
            flops=queries.size, bytes_accessed=8 * queries.size, transcendentals=0
        ),
    )(queries, out_grad)


def tick_kernel(tick, arrays, *refs):
    order_ref, q_ref, g_ref = refs[:3]
    outs = refs[3 + arrays :]
    dq_ref, near_out_ref, far_out_ref, s_ref, e_ref, dp_ref, ds_ref, acc_ref, kt_ref = outs
    local_rows, model = dq_ref.shape
    head_dim = near_out_ref.shape[1] // 2
    half_rows = near_out_ref.shape[0]
    kv_refs = [
        ref.at[pl.ds(row, local_rows)]
        for ref in refs[3 : 3 + arrays]
        for row in range(0, ref.shape[0], local_rows)
    ]
    blocks = len(kv_refs)
    heads = model // head_dim
    pairs = heads // 2
    width = 2 * local_rows
    chips = blocks // 2
    scale = 1.0 / math.sqrt(head_dim)
    exp_scale = scale * math.log2(math.e)

    core = lax.axis_index("core")
    chip = lax.axis_index("z")
    own_group = order_ref[2 * chip + core]

    def allowed(slot):
        source = jnp.bitwise_xor(chip, slot % chips)
        parity = core if slot < chips else 1 - core
        return order_ref[2 * source + parity] < own_group

    for slot in range(blocks):
        kt_ref[:, slot * local_rows : (slot + 1) * local_rows] = kv_refs[slot][:, :head_dim].T

    def pair_of(ref, pair):
        return ref[pl.ds((tick * pairs + pair) * width, width), :]

    def rows_of(slot):
        return slice(slot * local_rows, (slot + 1) * local_rows)

    def products(pair, slot):
        for out, ref, lo in ((s_ref, q_ref, 0), (dp_ref, g_ref, head_dim)):
            out[pair, rows_of(slot)] = lax.dot_general(
                kv_refs[slot][:, lo : lo + head_dim],
                pair_of(ref, pair),
                CONTRACT_LAST,
                preferred_element_type=jnp.float32,
            )

    def exponentials(pair, slot):
        scores = s_ref[pair, rows_of(slot)]
        if slot == 0:
            key_row = lax.broadcasted_iota(jnp.int32, (local_rows, width), 0)
            query_row = lax.rem(
                lax.broadcasted_iota(jnp.int32, (local_rows, width), 1), local_rows
            )
            scores = jnp.where(key_row <= query_row, scores, MASK_FILL)
        peak = jnp.max(scores, axis=0, keepdims=True) * exp_scale
        expo = jnp.exp2(scores * exp_scale - peak)
        e_ref[pair, rows_of(slot)] = expo
        total = jnp.sum(expo, axis=0, keepdims=True)
        weighted = jnp.sum(expo * dp_ref[pair, rows_of(slot)], axis=0, keepdims=True)
        if slot > 0:
            peak = jnp.where(allowed(slot), peak, MASK_FILL)
        return peak, total, weighted

    def combined(parts):
        biggest = parts[0][0]
        for peak, _, _ in parts[1:]:
            biggest = jnp.maximum(biggest, peak)
        factors = [jnp.exp2(peak - biggest) for peak, _, _ in parts]
        total = sum(part[1] * factor for part, factor in zip(parts, factors))
        weighted = sum(part[2] * factor for part, factor in zip(parts, factors))
        inverse = 1.0 / total
        return [factor * inverse for factor in factors], weighted * inverse

    def gradients(pair, slot, factors, delta):
        rows = rows_of(slot)
        probs = e_ref[pair, rows] * factors[slot]
        score_grad = (probs * (dp_ref[pair, rows] - delta)).astype(jnp.bfloat16)
        ds_ref[pair, rows] = score_grad
        key_terms = jnp.dot(score_grad, pair_of(q_ref, pair), preferred_element_type=jnp.float32)
        value_terms = jnp.dot(
            probs.astype(jnp.bfloat16), pair_of(g_ref, pair), preferred_element_type=jnp.float32
        )
        if pair > 0:
            key_terms += acc_ref[rows, :head_dim]
            value_terms += acc_ref[rows, head_dim:]
        if pair < pairs - 1:
            acc_ref[rows, :head_dim] = key_terms
            acc_ref[rows, head_dim:] = value_terms
        else:
            out = near_out_ref if slot < chips else far_out_ref
            place = rows_of(slot % chips)
            out[place, :head_dim] = (key_terms * scale).astype(out.dtype)
            out[place, head_dim:] = value_terms.astype(out.dtype)

    def query_grad(pair):
        query_t = jnp.dot(kt_ref[...], ds_ref[pair], preferred_element_type=jnp.float32)
        for half in range(2):
            lo = (2 * pair + half) * head_dim
            dq_ref[:, lo : lo + head_dim] = (
                query_t[:, half * local_rows : (half + 1) * local_rows].T * scale
            ).astype(dq_ref.dtype)

    held = None
    for pair in range(pairs + 1):
        parts = []
        if pair < pairs:
            products(pair, 0)
        for slot in range(blocks):
            if pair < pairs and slot + 1 < blocks:
                products(pair, slot + 1)
            if pair < pairs:
                parts.append(exponentials(pair, slot))
            if pair > 0:
                gradients(pair - 1, slot, *held)
            if pair > 1 and slot == 1:
                query_grad(pair - 2)
        if pair < pairs:
            held = combined(parts)
    query_grad(pairs - 1)


def attend_back(tick, group_order, queries, q_stack, g_stack, kv_arrays):
    local_rows, model = queries.shape[2:]
    width = kv_arrays[0].shape[1]
    key_rows = sum(array.shape[0] for array in kv_arrays)
    head_dim = width // 2
    pairs = model // head_dim // 2
    in_vmem = pl.BlockSpec(memory_space=pltpu.VMEM)
    tile = (pairs, key_rows, 2 * local_rows)

    def kernel(*refs):
        tick_kernel(tick, len(kv_arrays), *refs)

    return pl.pallas_call(
        kernel,
        out_shape=(
            jax.ShapeDtypeStruct((local_rows, model), jnp.bfloat16),
            jax.ShapeDtypeStruct((key_rows // 2, width), jnp.float32),
            jax.ShapeDtypeStruct((key_rows // 2, width), jnp.bfloat16),
        ),
        in_specs=[pl.BlockSpec(memory_space=pltpu.SMEM), *[in_vmem] * (2 + len(kv_arrays))],
        out_specs=(in_vmem, in_vmem, in_vmem),
        scratch_shapes=[
            pltpu.VMEM(tile, jnp.float32),
            pltpu.VMEM(tile, jnp.float32),
            pltpu.VMEM(tile, jnp.float32),
            pltpu.VMEM(tile, jnp.bfloat16),
            pltpu.VMEM((key_rows, width), jnp.float32),
            pltpu.VMEM((head_dim, key_rows), jnp.bfloat16),
        ],
        compiler_params=pltpu.CompilerParams(vmem_limit_bytes=44 * 2**20),
        cost_estimate=pl.CostEstimate(
            flops=40 * model * key_rows * local_rows,
            bytes_accessed=6 * local_rows * model + 5 * key_rows * width,
            transcendentals=model // head_dim * key_rows * local_rows,
        ),
    )(group_order, q_stack, g_stack, *kv_arrays)


def other_core(block):
    return lax.ppermute(block, "core", [(0, 1), (1, 0)])


def across_chips(block, k):
    return lax.ppermute(block, "z", [(chip, chip ^ k) for chip in range(lax.axis_size("z"))])


def section_swap(block, first):
    sections = lax.axis_size("section")
    route = []
    for low in range(first, sections, 2):
        high = (low + 1) % sections
        route += [(low, high), (high, low)]
    return lax.ppermute(block, "section", route)


def body(
    queries,
    out_grad,
    keys,
    values,
    entering_keys,
    entering_values,
    key_grads_in,
    value_grads_in,
    group_order,
):
    local_rows, head_dim = keys.shape[1:]
    width = 2 * head_dim
    chips = lax.axis_size("z")
    sections = lax.axis_size("section")
    section = lax.axis_index("section")

    own_pair = jnp.concatenate([keys[0], values[0]], axis=1)
    entering_pair = jnp.concatenate([entering_keys, entering_values], axis=1)
    leaving_pair = jnp.where(section == 0, entering_pair, own_pair)

    partners = range(chips - 1, 0, -1)
    near = [across_chips(own_pair, k) for k in partners][::-1]
    own_far = other_core(own_pair)
    next_pair = lax.ppermute(
        leaving_pair, "section", [(i, (i - 1) % sections) for i in range(sections)]
    )
    stacks = stacked_heads(queries, out_grad, head_dim)
    near, next_pair, stacks = lax.optimization_barrier((near, next_pair, stacks))
    far = [own_far] + [other_core(block) for block in near]
    next_near = [across_chips(next_pair, k) for k in partners][::-1]
    first_query, near_terms, far_terms = attend_back(
        0, group_order, queries, *stacks, [own_pair, *near, *far]
    )
    far_terms, next_near = lax.optimization_barrier((far_terms, [next_pair, *next_near]))
    next_kv = [*next_near, other_core(jnp.concatenate(next_near, axis=0))]

    def chip_sums(near_terms, far_terms):
        sums = near_terms + other_core(far_terms).astype(jnp.float32)
        sums = sums.reshape(chips, local_rows, width)
        return sums[0], [sums[k].astype(jnp.bfloat16) for k in range(1, chips)]

    def reduced(own_sum, leaving):
        for k in partners:
            own_sum = own_sum + across_chips(leaving[k - 1], k).astype(jnp.float32)
        return own_sum

    own_sum, leaving = chip_sums(near_terms, far_terms)
    stacks, leaving = lax.optimization_barrier((stacks, leaving))
    first_acc = jnp.concatenate([key_grads_in[0], value_grads_in[0]], axis=1) + reduced(
        own_sum, leaving
    )
    second_query, near_terms, far_terms = attend_back(1, group_order, queries, *stacks, next_kv)
    first_acc, far_terms = lax.optimization_barrier((first_acc, far_terms))
    early_acc = section_swap(first_acc, 0)
    own_sum, leaving = chip_sums(near_terms, far_terms)
    late_acc, leaving = lax.optimization_barrier((first_acc.astype(jnp.bfloat16), leaving))
    own_sum, queries_both = lax.optimization_barrier((own_sum, (first_query, second_query)))
    second_acc = reduced(own_sum, leaving)
    late_acc = section_swap(late_acc, 1).astype(jnp.float32)
    moved_acc = jnp.where(section % 2 == 0, early_acc, late_acc)
    second_acc = second_acc + jnp.where(section == sections - 1, 0.0, moved_acc)
    query_grads = jnp.stack(queries_both, axis=0)[:, None]
    key_grads = jnp.stack([first_acc[:, :head_dim], second_acc[:, :head_dim]], axis=0)[:, None]
    value_grads = jnp.stack([first_acc[:, head_dim:], second_acc[:, head_dim:]], axis=0)[:, None]
    return (query_grads, key_grads, value_grads)


def solution(mesh):
    sections, ctx_count = mesh.shape["section"], mesh.shape["ctx"]
    chip_mesh = jax.sharding.Mesh(
        mesh.devices.reshape(sections, ctx_count // 2, 2), ("section", "z", "core")
    )
    tokens = ("z", "core")
    return jax.shard_map(
        body,
        mesh=chip_mesh,
        in_specs=(
            P(None, "section", tokens, None),
            P(None, "section", tokens, None),
            P("section", tokens, None),
            P("section", tokens, None),
            P(tokens, None),
            P(tokens, None),
            P("section", tokens, None),
            P("section", tokens, None),
            P(),
        ),
        out_specs=(
            P(None, "section", tokens, None),
            P(None, "section", tokens, None),
            P(None, "section", tokens, None),
        ),
        check_vma=False,
    )
```

```python
import math

import jax
import jax.numpy as jnp
from jax import lax
from jax.experimental import pallas as pl
from jax.experimental.pallas import tpu as pltpu
from jax.sharding import PartitionSpec as P

MASK_FILL = -1e30
STRIP = 32
CONTRACT_LAST = (((1,), (1,)), ((), ()))


def block_places(chips):
    return [(k, same) for same in (True, False) for k in range(chips)]


def stack_kernel(order_ref, q_ref, g_ref, q_out_ref, g_out_ref, cap_ref):
    ticks, _, local_rows, model = q_ref.shape
    head_dim = q_out_ref.shape[1]
    heads = model // head_dim
    for tick in range(ticks):
        for head in range(heads):
            rows = pl.ds((tick * heads + head) * local_rows, local_rows)
            cols = pl.ds(head * head_dim, head_dim)
            q_out_ref[rows, :] = q_ref[tick, 0, :, cols]
            g_out_ref[rows, :] = g_ref[tick, 0, :, cols]
    chip, core = lax.axis_index("z"), lax.axis_index("core")
    own_group = order_ref[2 * chip + core]
    for slot, (k, same) in enumerate(block_places(cap_ref.shape[0] // 16)):
        source = 2 * jnp.bitwise_xor(chip, k) + (core if same else 1 - core)
        cap = jnp.where(order_ref[source] <= own_group, -MASK_FILL, MASK_FILL)
        cap_ref[slot * 8 : (slot + 1) * 8, :] = jnp.full((8, cap_ref.shape[1]), cap, jnp.float32)


def stacked_heads(group_order, queries, out_grad, head_dim):
    rows = queries.size // head_dim
    in_vmem = pl.BlockSpec(memory_space=pltpu.VMEM)
    stack = jax.ShapeDtypeStruct((rows, head_dim), queries.dtype)
    caps = jax.ShapeDtypeStruct((8 * group_order.size, 2 * queries.shape[2]), jnp.float32)
    return pl.pallas_call(
        stack_kernel,
        out_shape=(stack, stack, caps),
        in_specs=[pl.BlockSpec(memory_space=pltpu.SMEM), in_vmem, in_vmem],
        out_specs=(in_vmem, in_vmem, in_vmem),
        compiler_params=pltpu.CompilerParams(vmem_limit_bytes=8 * 2**20),
        cost_estimate=pl.CostEstimate(
            flops=queries.size, bytes_accessed=8 * queries.size, transcendentals=0
        ),
    )(group_order, queries, out_grad)


def tick_kernel(tick, arrays, *refs):
    q_ref, g_ref, cap_ref = refs[:3]
    outs = refs[3 + arrays :]
    dq_ref, near_out_ref, far_out_ref, s_ref, e_ref, dp_ref, *more = outs
    p_ref, ds_ref, acc_ref, kt_ref = more
    local_rows, model = dq_ref.shape
    head_dim = near_out_ref.shape[1] // 2
    half_rows = near_out_ref.shape[0]
    kv_refs = [
        ref.at[pl.ds(row, local_rows)]
        for ref in refs[3 : 3 + arrays]
        for row in range(0, ref.shape[0], local_rows)
    ]
    blocks = len(kv_refs)
    heads = model // head_dim
    pairs = heads // 2
    width = 2 * local_rows
    chips = blocks // 2
    scale = 1.0 / math.sqrt(head_dim)
    exp_scale = scale * math.log2(math.e)

    for slot in range(blocks):
        kt_ref[:, slot * local_rows : (slot + 1) * local_rows] = kv_refs[slot][:, :head_dim].T

    def pair_of(ref, pair):
        return ref[pl.ds((tick * pairs + pair) * width, width), :]

    def rows_of(slot):
        return slice(slot * local_rows, (slot + 1) * local_rows)

    def products(pair, slot):
        for out, ref, lo in ((s_ref, q_ref, 0), (dp_ref, g_ref, head_dim)):
            out[pair, rows_of(slot)] = lax.dot_general(
                kv_refs[slot][:, lo : lo + head_dim],
                pair_of(ref, pair),
                CONTRACT_LAST,
                preferred_element_type=jnp.float32,
            )

    def strips(slot):
        first = slot * local_rows
        return [slice(row, row + STRIP) for row in range(first, first + local_rows, STRIP)]

    def folded(strip, combine):
        return combine(strip.reshape(STRIP // 8, 8, width), axis=0)

    def exponentials(pair, slot):
        top = jnp.full((8, width), MASK_FILL, jnp.float32)
        for rows in strips(slot):
            scores = s_ref[pair, rows]
            if slot == 0:
                key_row = rows.start + lax.broadcasted_iota(jnp.int32, (STRIP, width), 0)
                query_row = lax.rem(
                    lax.broadcasted_iota(jnp.int32, (STRIP, width), 1), local_rows
                )
                scores = jnp.where(key_row <= query_row, scores, MASK_FILL)
                s_ref[pair, rows] = scores
            top = jnp.maximum(top, folded(scores, jnp.max))
        peak = jnp.max(top, axis=0, keepdims=True) * exp_scale
        total = jnp.zeros((8, width), jnp.float32)
        weighted = jnp.zeros((8, width), jnp.float32)
        for rows in strips(slot):
            expo = jnp.exp2(s_ref[pair, rows] * exp_scale - peak)
            e_ref[pair, rows] = expo
            total += folded(expo, jnp.sum)
            weighted += folded(expo * dp_ref[pair, rows], jnp.sum)
        if slot > 0:
            peak = jnp.minimum(peak, cap_ref[8 * slot : 8 * slot + 1, :])
        return (
            peak,
            jnp.sum(total, axis=0, keepdims=True),
            jnp.sum(weighted, axis=0, keepdims=True),
        )

    def combined(parts):
        biggest = parts[0][0]
        for peak, _, _ in parts[1:]:
            biggest = jnp.maximum(biggest, peak)
        factors = [jnp.exp2(peak - biggest) for peak, _, _ in parts]
        total = sum(part[1] * factor for part, factor in zip(parts, factors))
        weighted = sum(part[2] * factor for part, factor in zip(parts, factors))
        inverse = 1.0 / total
        return [factor * inverse for factor in factors], weighted * inverse

    def gradients(pair, slot, factors, delta):
        for rows in strips(slot):
            probs = e_ref[pair, rows] * factors[slot]
            p_ref[pair, rows] = probs.astype(jnp.bfloat16)
            ds_ref[pair, rows] = (probs * (dp_ref[pair, rows] - delta)).astype(jnp.bfloat16)
        rows = rows_of(slot)
        key_terms = jnp.dot(
            ds_ref[pair, rows], pair_of(q_ref, pair), preferred_element_type=jnp.float32
        )
        value_terms = jnp.dot(
            p_ref[pair, rows], pair_of(g_ref, pair), preferred_element_type=jnp.float32
        )
        if pair > 0:
            key_terms += acc_ref[rows, :head_dim]
            value_terms += acc_ref[rows, head_dim:]
        if pair < pairs - 1:
            acc_ref[rows, :head_dim] = key_terms
            acc_ref[rows, head_dim:] = value_terms
        else:
            out = near_out_ref if slot < chips else far_out_ref
            place = rows_of(slot % chips)
            out[place, :head_dim] = (key_terms * scale).astype(out.dtype)
            out[place, head_dim:] = value_terms.astype(out.dtype)

    def query_grad(pair):
        query_t = jnp.dot(kt_ref[...], ds_ref[pair], preferred_element_type=jnp.float32)
        for half in range(2):
            lo = (2 * pair + half) * head_dim
            dq_ref[:, lo : lo + head_dim] = (
                query_t[:, half * local_rows : (half + 1) * local_rows].T * scale
            ).astype(dq_ref.dtype)

    held = None
    for pair in range(pairs + 1):
        parts = []
        if pair < pairs:
            products(pair, 0)
        for slot in range(blocks):
            if pair < pairs and slot + 1 < blocks:
                products(pair, slot + 1)
            if pair < pairs:
                parts.append(exponentials(pair, slot))
            if pair > 0:
                gradients(pair - 1, slot, *held)
            if pair > 1 and slot == 1:
                query_grad(pair - 2)
        if pair < pairs:
            held = combined(parts)
    query_grad(pairs - 1)


def attend_back(tick, queries, stacks, kv_arrays):
    local_rows, model = queries.shape[2:]
    width = kv_arrays[0].shape[1]
    key_rows = sum(array.shape[0] for array in kv_arrays)
    head_dim = width // 2
    pairs = model // head_dim // 2
    in_vmem = pl.BlockSpec(memory_space=pltpu.VMEM)
    tile = (pairs, key_rows, 2 * local_rows)

    def kernel(*refs):
        tick_kernel(tick, len(kv_arrays), *refs)

    return pl.pallas_call(
        kernel,
        out_shape=(
            jax.ShapeDtypeStruct((local_rows, model), jnp.bfloat16),
            jax.ShapeDtypeStruct((key_rows // 2, width), jnp.float32),
            jax.ShapeDtypeStruct((key_rows // 2, width), jnp.bfloat16),
        ),
        in_specs=[in_vmem] * (3 + len(kv_arrays)),
        out_specs=(in_vmem, in_vmem, in_vmem),
        scratch_shapes=[
            pltpu.VMEM(tile, jnp.float32),
            pltpu.VMEM(tile, jnp.float32),
            pltpu.VMEM(tile, jnp.float32),
            pltpu.VMEM(tile, jnp.bfloat16),
            pltpu.VMEM(tile, jnp.bfloat16),
            pltpu.VMEM((key_rows, width), jnp.float32),
            pltpu.VMEM((head_dim, key_rows), jnp.bfloat16),
        ],
        compiler_params=pltpu.CompilerParams(vmem_limit_bytes=44 * 2**20),
        cost_estimate=pl.CostEstimate(
            flops=40 * model * key_rows * local_rows,
            bytes_accessed=6 * local_rows * model + 5 * key_rows * width,
            transcendentals=model // head_dim * key_rows * local_rows,
        ),
    )(*stacks, *kv_arrays)


def other_core(block):
    return lax.ppermute(block, "core", [(0, 1), (1, 0)])


def across_chips(block, k):
    return lax.ppermute(block, "z", [(chip, chip ^ k) for chip in range(lax.axis_size("z"))])


def section_swap(block, first):
    sections = lax.axis_size("section")
    route = []
    for low in range(first, sections, 2):
        high = (low + 1) % sections
        route += [(low, high), (high, low)]
    return lax.ppermute(block, "section", route)


def body(
    queries,
    out_grad,
    keys,
    values,
    entering_keys,
    entering_values,
    key_grads_in,
    value_grads_in,
    group_order,
):
    local_rows, head_dim = keys.shape[1:]
    width = 2 * head_dim
    chips = lax.axis_size("z")
    sections = lax.axis_size("section")
    section = lax.axis_index("section")

    own_pair = jnp.concatenate([keys[0], values[0]], axis=1)
    entering_pair = jnp.concatenate([entering_keys, entering_values], axis=1)
    leaving_pair = jnp.where(section == 0, entering_pair, own_pair)

    partners = range(chips - 1, 0, -1)
    near = [across_chips(own_pair, k) for k in partners][::-1]
    own_far = other_core(own_pair)
    next_pair = lax.ppermute(
        leaving_pair, "section", [(i, (i - 1) % sections) for i in range(sections)]
    )
    stacks = stacked_heads(group_order, queries, out_grad, head_dim)
    near, next_pair, stacks = lax.optimization_barrier((near, next_pair, stacks))
    far = [own_far] + [other_core(block) for block in near]
    next_near = [across_chips(next_pair, k) for k in partners][::-1]
    first_query, near_terms, far_terms = attend_back(0, queries, stacks, [own_pair, *near, *far])
    far_terms, next_near = lax.optimization_barrier((far_terms, [next_pair, *next_near]))
    next_kv = [*next_near, other_core(jnp.concatenate(next_near, axis=0))]

    def chip_sums(near_terms, far_terms):
        sums = near_terms + other_core(far_terms).astype(jnp.float32)
        sums = sums.reshape(chips, local_rows, width)
        return sums[0], [sums[k].astype(jnp.bfloat16) for k in range(1, chips)]

    def reduced(own_sum, leaving):
        for k in partners:
            own_sum = own_sum + across_chips(leaving[k - 1], k).astype(jnp.float32)
        return own_sum

    own_sum, leaving = chip_sums(near_terms, far_terms)
    stacks, leaving = lax.optimization_barrier((stacks, leaving))
    first_acc = jnp.concatenate([key_grads_in[0], value_grads_in[0]], axis=1) + reduced(
        own_sum, leaving
    )
    second_query, near_terms, far_terms = attend_back(1, queries, stacks, next_kv)
    first_acc, far_terms = lax.optimization_barrier((first_acc, far_terms))
    early_acc = section_swap(first_acc, 0)
    own_sum, leaving = chip_sums(near_terms, far_terms)
    late_acc, leaving = lax.optimization_barrier((first_acc.astype(jnp.bfloat16), leaving))
    own_sum, queries_both = lax.optimization_barrier((own_sum, (first_query, second_query)))
    second_acc = reduced(own_sum, leaving)
    late_acc = section_swap(late_acc, 1).astype(jnp.float32)
    moved_acc = jnp.where(section % 2 == 0, early_acc, late_acc)
    second_acc = second_acc + jnp.where(section == sections - 1, 0.0, moved_acc)
    query_grads = jnp.stack(queries_both, axis=0)[:, None]
    key_grads = jnp.stack([first_acc[:, :head_dim], second_acc[:, :head_dim]], axis=0)[:, None]
    value_grads = jnp.stack([first_acc[:, head_dim:], second_acc[:, head_dim:]], axis=0)[:, None]
    return (query_grads, key_grads, value_grads)


def solution(mesh):
    sections, ctx_count = mesh.shape["section"], mesh.shape["ctx"]
    chip_mesh = jax.sharding.Mesh(
        mesh.devices.reshape(sections, ctx_count // 2, 2), ("section", "z", "core")
    )
    tokens = ("z", "core")
    return jax.shard_map(
        body,
        mesh=chip_mesh,
        in_specs=(
            P(None, "section", tokens, None),
            P(None, "section", tokens, None),
            P("section", tokens, None),
            P("section", tokens, None),
            P(tokens, None),
            P(tokens, None),
            P("section", tokens, None),
            P("section", tokens, None),
            P(),
        ),
        out_specs=(
            P(None, "section", tokens, None),
            P(None, "section", tokens, None),
            P(None, "section", tokens, None),
        ),
        check_vma=False,
    )
```

```python
import math

import jax
import jax.numpy as jnp
from jax import lax
from jax.experimental import pallas as pl
from jax.experimental.pallas import tpu as pltpu
from jax.sharding import PartitionSpec as P

MASK_FILL = -1e30
STRIP = 32
CONTRACT_LAST = (((1,), (1,)), ((), ()))


def block_places(chips):
    return [(k, same) for same in (True, False) for k in range(chips)]


def stack_kernel(order_ref, q_ref, g_ref, q_out_ref, g_out_ref, cap_ref):
    ticks, _, local_rows, model = q_ref.shape
    head_dim = q_out_ref.shape[1]
    heads = model // head_dim
    for tick in range(ticks):
        for head in range(heads):
            rows = pl.ds((tick * heads + head) * local_rows, local_rows)
            cols = pl.ds(head * head_dim, head_dim)
            q_out_ref[rows, :] = q_ref[tick, 0, :, cols]
            g_out_ref[rows, :] = g_ref[tick, 0, :, cols]
    chip, core = lax.axis_index("z"), lax.axis_index("core")
    own_group = order_ref[2 * chip + core]
    for slot, (k, same) in enumerate(block_places(cap_ref.shape[0] // 16)):
        source = 2 * jnp.bitwise_xor(chip, k) + (core if same else 1 - core)
        cap = jnp.where(order_ref[source] <= own_group, -MASK_FILL, MASK_FILL)
        cap_ref[slot * 8 : (slot + 1) * 8, :] = jnp.full((8, cap_ref.shape[1]), cap, jnp.float32)


def stacked_heads(group_order, queries, out_grad, head_dim):
    rows = queries.size // head_dim
    in_vmem = pl.BlockSpec(memory_space=pltpu.VMEM)
    stack = jax.ShapeDtypeStruct((rows, head_dim), queries.dtype)
    caps = jax.ShapeDtypeStruct((8 * group_order.size, 2 * queries.shape[2]), jnp.float32)
    return pl.pallas_call(
        stack_kernel,
        out_shape=(stack, stack, caps),
        in_specs=[pl.BlockSpec(memory_space=pltpu.SMEM), in_vmem, in_vmem],
        out_specs=(in_vmem, in_vmem, in_vmem),
        compiler_params=pltpu.CompilerParams(vmem_limit_bytes=8 * 2**20),
        cost_estimate=pl.CostEstimate(
            flops=queries.size, bytes_accessed=8 * queries.size, transcendentals=0
        ),
    )(group_order, queries, out_grad)


def tick_kernel(tick, arrays, *refs):
    q_ref, g_ref, cap_ref = refs[:3]
    outs = refs[3 + arrays :]
    dq_ref, near_out_ref, far_out_ref, s_ref, e_ref, dp_ref, *more = outs
    p_ref, ds_ref, acc_ref, kt_ref = more
    local_rows, model = dq_ref.shape
    head_dim = near_out_ref.shape[1] // 2
    half_rows = near_out_ref.shape[0]
    kv_refs = [
        ref.at[pl.ds(row, local_rows)]
        for ref in refs[3 : 3 + arrays]
        for row in range(0, ref.shape[0], local_rows)
    ]
    blocks = len(kv_refs)
    heads = model // head_dim
    pairs = heads // 2
    width = 2 * local_rows
    chips = blocks // 2
    scale = 1.0 / math.sqrt(head_dim)
    exp_scale = scale * math.log2(math.e)

    for slot in range(blocks):
        kt_ref[:, slot * local_rows : (slot + 1) * local_rows] = kv_refs[slot][:, :head_dim].T

    def pair_of(ref, pair):
        return ref[pl.ds((tick * pairs + pair) * width, width), :]

    def rows_of(slot):
        return slice(slot * local_rows, (slot + 1) * local_rows)

    def products(pair, slot):
        for out, ref, lo in ((s_ref, q_ref, 0), (dp_ref, g_ref, head_dim)):
            out[pair, rows_of(slot)] = lax.dot_general(
                kv_refs[slot][:, lo : lo + head_dim],
                pair_of(ref, pair),
                CONTRACT_LAST,
                preferred_element_type=jnp.float32,
            )

    def strips(slot):
        first = slot * local_rows
        return [slice(row, row + STRIP) for row in range(first, first + local_rows, STRIP)]

    def folded(strip, combine):
        return combine(strip.reshape(STRIP // 8, 8, width), axis=0)

    def exponentials(pair, slot):
        top = jnp.full((8, width), MASK_FILL, jnp.float32)
        for rows in strips(slot):
            scores = s_ref[pair, rows]
            if slot == 0:
                key_row = rows.start + lax.broadcasted_iota(jnp.int32, (STRIP, width), 0)
                query_row = lax.rem(
                    lax.broadcasted_iota(jnp.int32, (STRIP, width), 1), local_rows
                )
                scores = jnp.where(key_row <= query_row, scores, MASK_FILL)
                s_ref[pair, rows] = scores
            top = jnp.maximum(top, folded(scores, jnp.max))
        peak = jnp.max(top, axis=0, keepdims=True) * exp_scale
        total = jnp.zeros((8, width), jnp.float32)
        weighted = jnp.zeros((8, width), jnp.float32)
        for rows in strips(slot):
            expo = jnp.exp2(s_ref[pair, rows] * exp_scale - peak)
            e_ref[pair, rows] = expo
            total += folded(expo, jnp.sum)
            weighted += folded(expo * dp_ref[pair, rows], jnp.sum)
        if slot > 0:
            peak = jnp.minimum(peak, cap_ref[8 * slot : 8 * slot + 1, :])
        return (
            peak,
            jnp.sum(total, axis=0, keepdims=True),
            jnp.sum(weighted, axis=0, keepdims=True),
        )

    def combined(parts):
        biggest = parts[0][0]
        for peak, _, _ in parts[1:]:
            biggest = jnp.maximum(biggest, peak)
        factors = [jnp.exp2(peak - biggest) for peak, _, _ in parts]
        total = sum(part[1] * factor for part, factor in zip(parts, factors))
        weighted = sum(part[2] * factor for part, factor in zip(parts, factors))
        inverse = 1.0 / total
        return [factor * inverse for factor in factors], weighted * inverse

    def gradients(pair, slot, factors, delta):
        for rows in strips(slot):
            probs = e_ref[pair, rows] * factors[slot]
            p_ref[pair, rows] = probs.astype(jnp.bfloat16)
            ds_ref[pair, rows] = (probs * (dp_ref[pair, rows] - delta)).astype(jnp.bfloat16)
        rows = rows_of(slot)
        key_terms = jnp.dot(
            ds_ref[pair, rows], pair_of(q_ref, pair), preferred_element_type=jnp.float32
        )
        value_terms = jnp.dot(
            p_ref[pair, rows], pair_of(g_ref, pair), preferred_element_type=jnp.float32
        )
        if pair > 0:
            key_terms += acc_ref[rows, :head_dim]
            value_terms += acc_ref[rows, head_dim:]
        if pair < pairs - 1:
            acc_ref[rows, :head_dim] = key_terms
            acc_ref[rows, head_dim:] = value_terms
        else:
            out = near_out_ref if slot < chips else far_out_ref
            place = rows_of(slot % chips)
            out[place, :head_dim] = (key_terms * scale).astype(out.dtype)
            out[place, head_dim:] = value_terms.astype(out.dtype)

    def query_grad(pair):
        query_t = jnp.dot(kt_ref[...], ds_ref[pair], preferred_element_type=jnp.float32)
        for half in range(2):
            lo = (2 * pair + half) * head_dim
            dq_ref[:, lo : lo + head_dim] = (
                query_t[:, half * local_rows : (half + 1) * local_rows].T * scale
            ).astype(dq_ref.dtype)

    held = None
    for pair in range(pairs + 1):
        parts = []
        if pair < pairs:
            products(pair, 0)
        for slot in range(blocks):
            if pair < pairs and slot + 1 < blocks:
                products(pair, slot + 1)
            if pair < pairs:
                parts.append(exponentials(pair, slot))
            if pair > 0:
                gradients(pair - 1, slot, *held)
            if pair > 1 and slot == 1:
                query_grad(pair - 2)
        if pair < pairs:
            held = combined(parts)
    query_grad(pairs - 1)


def attend_back(tick, queries, stacks, kv_arrays):
    local_rows, model = queries.shape[2:]
    width = kv_arrays[0].shape[1]
    key_rows = sum(array.shape[0] for array in kv_arrays)
    head_dim = width // 2
    pairs = model // head_dim // 2
    in_vmem = pl.BlockSpec(memory_space=pltpu.VMEM)
    tile = (pairs, key_rows, 2 * local_rows)

    def kernel(*refs):
        tick_kernel(tick, len(kv_arrays), *refs)

    return pl.pallas_call(
        kernel,
        out_shape=(
            jax.ShapeDtypeStruct((local_rows, model), jnp.bfloat16),
            jax.ShapeDtypeStruct((key_rows // 2, width), jnp.float32),
            jax.ShapeDtypeStruct((key_rows // 2, width), jnp.bfloat16),
        ),
        in_specs=[in_vmem] * (3 + len(kv_arrays)),
        out_specs=(in_vmem, in_vmem, in_vmem),
        scratch_shapes=[
            pltpu.VMEM(tile, jnp.float32),
            pltpu.VMEM(tile, jnp.float32),
            pltpu.VMEM(tile, jnp.float32),
            pltpu.VMEM(tile, jnp.bfloat16),
            pltpu.VMEM(tile, jnp.bfloat16),
            pltpu.VMEM((key_rows, width), jnp.float32),
            pltpu.VMEM((head_dim, key_rows), jnp.bfloat16),
        ],
        compiler_params=pltpu.CompilerParams(vmem_limit_bytes=44 * 2**20),
        cost_estimate=pl.CostEstimate(
            flops=40 * model * key_rows * local_rows,
            bytes_accessed=6 * local_rows * model + 5 * key_rows * width,
            transcendentals=model // head_dim * key_rows * local_rows,
        ),
    )(*stacks, *kv_arrays)


def other_core(block):
    return lax.ppermute(block, "core", [(0, 1), (1, 0)])


def across_chips(block, k):
    return lax.ppermute(block, "z", [(chip, chip ^ k) for chip in range(lax.axis_size("z"))])


def section_swap(block, first):
    sections = lax.axis_size("section")
    route = []
    for low in range(first, sections, 2):
        high = (low + 1) % sections
        route += [(low, high), (high, low)]
    return lax.ppermute(block, "section", route)


def body(
    queries,
    out_grad,
    keys,
    values,
    entering_keys,
    entering_values,
    key_grads_in,
    value_grads_in,
    group_order,
):
    local_rows, head_dim = keys.shape[1:]
    width = 2 * head_dim
    chips = lax.axis_size("z")
    sections = lax.axis_size("section")
    section = lax.axis_index("section")

    own_pair = jnp.concatenate([keys[0], values[0]], axis=1)
    entering_pair = jnp.concatenate([entering_keys, entering_values], axis=1)
    leaving_pair = jnp.where(section == 0, entering_pair, own_pair)

    partners = range(chips - 1, 0, -1)
    near = [across_chips(own_pair, k) for k in partners][::-1]
    own_far = other_core(own_pair)
    next_pair = lax.ppermute(
        leaving_pair, "section", [(i, (i - 1) % sections) for i in range(sections)]
    )
    stacks = stacked_heads(group_order, queries, out_grad, head_dim)
    near, next_pair, stacks = lax.optimization_barrier((near, next_pair, stacks))
    far = [own_far] + [other_core(block) for block in near]
    next_near = [across_chips(next_pair, k) for k in partners][::-1]
    first_query, near_terms, far_terms = attend_back(0, queries, stacks, [own_pair, *near, *far])
    far_terms, next_near = lax.optimization_barrier((far_terms, [next_pair, *next_near]))
    next_kv = [*next_near, other_core(jnp.concatenate(next_near, axis=0))]

    def chip_sums(near_terms, received):
        sums = near_terms + received.astype(jnp.float32)
        sums = sums.reshape(chips, local_rows, width)
        return sums[0], [sums[k].astype(jnp.bfloat16) for k in range(1, chips)]

    def reduced(own_sum, leaving):
        for k in partners:
            own_sum = own_sum + across_chips(leaving[k - 1], k).astype(jnp.float32)
        return own_sum

    own_sum, leaving = chip_sums(near_terms, other_core(far_terms))
    stacks, leaving = lax.optimization_barrier((stacks, leaving))
    first_acc = jnp.concatenate([key_grads_in[0], value_grads_in[0]], axis=1) + reduced(
        own_sum, leaving
    )
    second_query, near_terms, far_terms = attend_back(1, queries, stacks, next_kv)
    received = other_core(far_terms)
    first_acc, received = lax.optimization_barrier((first_acc, received))
    own_sum, leaving = chip_sums(near_terms, received)
    is_odd = section % 2 == 1
    late_acc = first_acc.astype(jnp.bfloat16)
    odd_acc = jnp.where(is_odd, late_acc, 0)
    even_acc = jnp.where(is_odd | (section == 0), 0, late_acc)
    odd_acc, even_acc, leaving = lax.optimization_barrier((odd_acc, even_acc, leaving))
    own_sum, queries_both = lax.optimization_barrier((own_sum, (first_query, second_query)))
    second_acc = reduced(own_sum, leaving)
    second_acc = second_acc + section_swap(odd_acc, 0).astype(jnp.float32)
    second_acc = second_acc + section_swap(even_acc, 1).astype(jnp.float32)
    query_grads = jnp.stack(queries_both, axis=0)[:, None]
    key_grads = jnp.stack([first_acc[:, :head_dim], second_acc[:, :head_dim]], axis=0)[:, None]
    value_grads = jnp.stack([first_acc[:, head_dim:], second_acc[:, head_dim:]], axis=0)[:, None]
    return (query_grads, key_grads, value_grads)


def solution(mesh):
    sections, ctx_count = mesh.shape["section"], mesh.shape["ctx"]
    chip_mesh = jax.sharding.Mesh(
        mesh.devices.reshape(sections, ctx_count // 2, 2), ("section", "z", "core")
    )
    tokens = ("z", "core")
    return jax.shard_map(
        body,
        mesh=chip_mesh,
        in_specs=(
            P(None, "section", tokens, None),
            P(None, "section", tokens, None),
            P("section", tokens, None),
            P("section", tokens, None),
            P(tokens, None),
            P(tokens, None),
            P("section", tokens, None),
            P("section", tokens, None),
            P(),
        ),
        out_specs=(
            P(None, "section", tokens, None),
            P(None, "section", tokens, None),
            P(None, "section", tokens, None),
        ),
        check_vma=False,
    )
```

```python
import math

import jax
import jax.numpy as jnp
from jax import lax
from jax.experimental import pallas as pl
from jax.experimental.pallas import tpu as pltpu
from jax.sharding import PartitionSpec as P

MASK_FILL = -1e30
STRIP = 32
CONTRACT_LAST = (((1,), (1,)), ((), ()))


def block_places(chips):
    return [(k, same) for same in (True, False) for k in range(chips)]


def stack_kernel(order_ref, q_ref, g_ref, q_out_ref, g_out_ref, cap_ref):
    ticks, _, local_rows, model = q_ref.shape
    head_dim = q_out_ref.shape[1]
    heads = model // head_dim
    for tick in range(ticks):
        for head in range(heads):
            rows = pl.ds((tick * heads + head) * local_rows, local_rows)
            cols = pl.ds(head * head_dim, head_dim)
            q_out_ref[rows, :] = q_ref[tick, 0, :, cols]
            g_out_ref[rows, :] = g_ref[tick, 0, :, cols]
    chip, core = lax.axis_index("z"), lax.axis_index("core")
    own_group = order_ref[2 * chip + core]
    for slot, (k, same) in enumerate(block_places(cap_ref.shape[0] // 16)):
        source = 2 * jnp.bitwise_xor(chip, k) + (core if same else 1 - core)
        cap = jnp.where(order_ref[source] <= own_group, -MASK_FILL, MASK_FILL)
        cap_ref[slot * 8 : (slot + 1) * 8, :] = jnp.full((8, cap_ref.shape[1]), cap, jnp.float32)


def stacked_heads(group_order, queries, out_grad, head_dim):
    rows = queries.size // head_dim
    in_vmem = pl.BlockSpec(memory_space=pltpu.VMEM)
    stack = jax.ShapeDtypeStruct((rows, head_dim), queries.dtype)
    caps = jax.ShapeDtypeStruct((8 * group_order.size, 2 * queries.shape[2]), jnp.float32)
    return pl.pallas_call(
        stack_kernel,
        out_shape=(stack, stack, caps),
        in_specs=[pl.BlockSpec(memory_space=pltpu.SMEM), in_vmem, in_vmem],
        out_specs=(in_vmem, in_vmem, in_vmem),
        compiler_params=pltpu.CompilerParams(vmem_limit_bytes=8 * 2**20),
        cost_estimate=pl.CostEstimate(
            flops=queries.size, bytes_accessed=8 * queries.size, transcendentals=0
        ),
    )(group_order, queries, out_grad)


def tick_kernel(tick, arrays, *refs):
    q_ref, g_ref, cap_ref = refs[:3]
    outs = refs[3 + arrays :]
    dq_ref, near_out_ref, far_out_ref, s_ref, e_ref, dp_ref, *more = outs
    p_ref, ds_ref, acc_ref, kt_ref = more
    local_rows, model = dq_ref.shape
    head_dim = near_out_ref.shape[1] // 2
    half_rows = near_out_ref.shape[0]
    kv_refs = [
        ref.at[pl.ds(row, local_rows)]
        for ref in refs[3 : 3 + arrays]
        for row in range(0, ref.shape[0], local_rows)
    ]
    blocks = len(kv_refs)
    heads = model // head_dim
    pairs = heads // 2
    width = 2 * local_rows
    chips = blocks // 2
    scale = 1.0 / math.sqrt(head_dim)
    exp_scale = scale * math.log2(math.e)

    for slot in range(blocks):
        kt_ref[:, slot * local_rows : (slot + 1) * local_rows] = kv_refs[slot][:, :head_dim].T

    def pair_of(ref, pair):
        return ref[pl.ds((tick * pairs + pair) * width, width), :]

    def rows_of(slot):
        return slice(slot * local_rows, (slot + 1) * local_rows)

    def products(pair, slot):
        for out, ref, lo in ((s_ref, q_ref, 0), (dp_ref, g_ref, head_dim)):
            out[pair, rows_of(slot)] = lax.dot_general(
                kv_refs[slot][:, lo : lo + head_dim],
                pair_of(ref, pair),
                CONTRACT_LAST,
                preferred_element_type=jnp.float32,
            )

    def strips(slot):
        first = slot * local_rows
        return [slice(row, row + STRIP) for row in range(first, first + local_rows, STRIP)]

    def folded(strip, combine):
        return combine(strip.reshape(STRIP // 8, 8, width), axis=0)

    def exponentials(pair, slot):
        top = jnp.full((8, width), MASK_FILL, jnp.float32)
        for rows in strips(slot):
            scores = s_ref[pair, rows]
            if slot == 0:
                key_row = rows.start + lax.broadcasted_iota(jnp.int32, (STRIP, width), 0)
                query_row = lax.rem(
                    lax.broadcasted_iota(jnp.int32, (STRIP, width), 1), local_rows
                )
                scores = jnp.where(key_row <= query_row, scores, MASK_FILL)
                s_ref[pair, rows] = scores
            top = jnp.maximum(top, folded(scores, jnp.max))
        peak = jnp.max(top, axis=0, keepdims=True) * exp_scale
        total = jnp.zeros((8, width), jnp.float32)
        weighted = jnp.zeros((8, width), jnp.float32)
        for rows in strips(slot):
            expo = jnp.exp2(s_ref[pair, rows] * exp_scale - peak)
            e_ref[pair, rows] = expo
            total += folded(expo, jnp.sum)
            weighted += folded(expo * dp_ref[pair, rows], jnp.sum)
        if slot > 0:
            peak = jnp.minimum(peak, cap_ref[8 * slot : 8 * slot + 1, :])
        return (
            peak,
            jnp.sum(total, axis=0, keepdims=True),
            jnp.sum(weighted, axis=0, keepdims=True),
        )

    def combined(parts):
        biggest = parts[0][0]
        for peak, _, _ in parts[1:]:
            biggest = jnp.maximum(biggest, peak)
        factors = [jnp.exp2(peak - biggest) for peak, _, _ in parts]
        total = sum(part[1] * factor for part, factor in zip(parts, factors))
        weighted = sum(part[2] * factor for part, factor in zip(parts, factors))
        inverse = 1.0 / total
        return [factor * inverse for factor in factors], weighted * inverse

    def gradients(pair, slot, factors, delta):
        for rows in strips(slot):
            probs = e_ref[pair, rows] * factors[slot]
            p_ref[pair, rows] = probs.astype(jnp.bfloat16)
            ds_ref[pair, rows] = (probs * (dp_ref[pair, rows] - delta)).astype(jnp.bfloat16)
        rows = rows_of(slot)
        key_terms = jnp.dot(
            ds_ref[pair, rows], pair_of(q_ref, pair), preferred_element_type=jnp.float32
        )
        value_terms = jnp.dot(
            p_ref[pair, rows], pair_of(g_ref, pair), preferred_element_type=jnp.float32
        )
        if pair > 0:
            key_terms += acc_ref[rows, :head_dim]
            value_terms += acc_ref[rows, head_dim:]
        if pair < pairs - 1:
            acc_ref[rows, :head_dim] = key_terms
            acc_ref[rows, head_dim:] = value_terms
        else:
            out = near_out_ref if slot < chips else far_out_ref
            place = rows_of(slot % chips)
            out[place, :head_dim] = (key_terms * scale).astype(out.dtype)
            out[place, head_dim:] = value_terms.astype(out.dtype)

    def query_grad(pair):
        query_t = jnp.dot(kt_ref[...], ds_ref[pair], preferred_element_type=jnp.float32)
        for half in range(2):
            lo = (2 * pair + half) * head_dim
            dq_ref[:, lo : lo + head_dim] = (
                query_t[:, half * local_rows : (half + 1) * local_rows].T * scale
            ).astype(dq_ref.dtype)

    held = None
    for pair in range(pairs + 1):
        parts = []
        if pair < pairs:
            products(pair, 0)
        for slot in range(blocks):
            if pair < pairs and slot + 1 < blocks:
                products(pair, slot + 1)
            if pair < pairs:
                parts.append(exponentials(pair, slot))
            if pair > 0:
                gradients(pair - 1, slot, *held)
            if pair > 1 and slot == 1:
                query_grad(pair - 2)
        if pair < pairs:
            held = combined(parts)
    query_grad(pairs - 1)


def attend_back(tick, queries, stacks, kv_arrays):
    local_rows, model = queries.shape[2:]
    width = kv_arrays[0].shape[1]
    key_rows = sum(array.shape[0] for array in kv_arrays)
    head_dim = width // 2
    pairs = model // head_dim // 2
    in_vmem = pl.BlockSpec(memory_space=pltpu.VMEM)
    tile = (pairs, key_rows, 2 * local_rows)

    def kernel(*refs):
        tick_kernel(tick, len(kv_arrays), *refs)

    return pl.pallas_call(
        kernel,
        out_shape=(
            jax.ShapeDtypeStruct((local_rows, model), jnp.bfloat16),
            jax.ShapeDtypeStruct((key_rows // 2, width), jnp.float32),
            jax.ShapeDtypeStruct((key_rows // 2, width), jnp.bfloat16),
        ),
        in_specs=[in_vmem] * (3 + len(kv_arrays)),
        out_specs=(in_vmem, in_vmem, in_vmem),
        scratch_shapes=[
            pltpu.VMEM(tile, jnp.float32),
            pltpu.VMEM(tile, jnp.float32),
            pltpu.VMEM(tile, jnp.float32),
            pltpu.VMEM(tile, jnp.bfloat16),
            pltpu.VMEM(tile, jnp.bfloat16),
            pltpu.VMEM((key_rows, width), jnp.float32),
            pltpu.VMEM((head_dim, key_rows), jnp.bfloat16),
        ],
        compiler_params=pltpu.CompilerParams(vmem_limit_bytes=44 * 2**20),
        cost_estimate=pl.CostEstimate(
            flops=40 * model * key_rows * local_rows,
            bytes_accessed=6 * local_rows * model + 5 * key_rows * width,
            transcendentals=model // head_dim * key_rows * local_rows,
        ),
    )(*stacks, *kv_arrays)


def finish_kernel(first_ref, own_ref, *refs):
    key_ref, value_ref, held, copy_sem = refs[-4:]
    head_dim = key_ref.shape[3]
    copies = []
    for tick in range(2):
        total = (first_ref if tick == 0 else own_ref)[...]
        if tick == 1:
            for ref in refs[:-4]:
                total = total + ref[...].astype(jnp.float32)
        for half, out in enumerate((key_ref, value_ref)):
            held[tick, half] = total[:, half * head_dim : (half + 1) * head_dim]
            copy = pltpu.make_async_copy(
                held.at[tick, half], out.at[tick, 0], copy_sem.at[2 * tick + half]
            )
            copy.start()
            copies.append(copy)
    for copy in copies:
        copy.wait()


def finished(first_acc, own_sum, blocks):
    rows, width = first_acc.shape
    head_dim = width // 2
    in_vmem = pl.BlockSpec(memory_space=pltpu.VMEM)
    return pl.pallas_call(
        finish_kernel,
        out_shape=(jax.ShapeDtypeStruct((2, 1, rows, head_dim), jnp.float32),) * 2,
        in_specs=[in_vmem] * (2 + len(blocks)),
        out_specs=(pl.BlockSpec(memory_space=pl.ANY),) * 2,
        scratch_shapes=[
            pltpu.VMEM((2, 2, rows, head_dim), jnp.float32),
            pltpu.SemaphoreType.DMA((4,)),
        ],
        compiler_params=pltpu.CompilerParams(vmem_limit_bytes=8 * 2**20),
        cost_estimate=pl.CostEstimate(
            flops=len(blocks) * first_acc.size,
            bytes_accessed=16 * first_acc.size,
            transcendentals=0,
        ),
    )(first_acc, own_sum, *blocks)


def other_core(block):
    return lax.ppermute(block, "core", [(0, 1), (1, 0)])


def across_chips(block, k):
    return lax.ppermute(block, "z", [(chip, chip ^ k) for chip in range(lax.axis_size("z"))])


def section_swap(block, first):
    sections = lax.axis_size("section")
    route = []
    for low in range(first, sections, 2):
        high = (low + 1) % sections
        route += [(low, high), (high, low)]
    return lax.ppermute(block, "section", route)


def body(
    queries,
    out_grad,
    keys,
    values,
    entering_keys,
    entering_values,
    key_grads_in,
    value_grads_in,
    group_order,
):
    local_rows, head_dim = keys.shape[1:]
    width = 2 * head_dim
    chips = lax.axis_size("z")
    sections = lax.axis_size("section")
    section = lax.axis_index("section")

    own_pair = jnp.concatenate([keys[0], values[0]], axis=1)
    entering_pair = jnp.concatenate([entering_keys, entering_values], axis=1)
    leaving_pair = jnp.where(section == 0, entering_pair, own_pair)

    partners = range(chips - 1, 0, -1)
    near = [across_chips(own_pair, k) for k in partners][::-1]
    own_far = other_core(own_pair)
    next_pair = lax.ppermute(
        leaving_pair, "section", [(i, (i - 1) % sections) for i in range(sections)]
    )
    stacks = stacked_heads(group_order, queries, out_grad, head_dim)
    near, next_pair, stacks = lax.optimization_barrier((near, next_pair, stacks))
    far = [own_far] + [other_core(block) for block in near]
    next_near = [across_chips(next_pair, k) for k in partners][::-1]
    first_query, near_terms, far_terms = attend_back(0, queries, stacks, [own_pair, *near, *far])
    far_terms, next_near = lax.optimization_barrier((far_terms, [next_pair, *next_near]))
    next_kv = [*next_near, other_core(jnp.concatenate(next_near, axis=0))]

    def chip_sums(near_terms, received):
        sums = near_terms + received.astype(jnp.float32)
        sums = sums.reshape(chips, local_rows, width)
        return sums[0], [sums[k].astype(jnp.bfloat16) for k in range(1, chips)]

    def reduced(own_sum, leaving):
        for k in partners:
            own_sum = own_sum + across_chips(leaving[k - 1], k).astype(jnp.float32)
        return own_sum

    own_sum, leaving = chip_sums(near_terms, other_core(far_terms))
    stacks, leaving = lax.optimization_barrier((stacks, leaving))
    first_acc = jnp.concatenate([key_grads_in[0], value_grads_in[0]], axis=1) + reduced(
        own_sum, leaving
    )
    second_query, near_terms, far_terms = attend_back(1, queries, stacks, next_kv)
    received = other_core(far_terms)
    first_acc, received = lax.optimization_barrier((first_acc, received))
    own_sum, leaving = chip_sums(near_terms, received)
    is_odd = section % 2 == 1
    late_acc = first_acc.astype(jnp.bfloat16)
    odd_acc = jnp.where(is_odd, late_acc, 0)
    even_acc = jnp.where(is_odd | (section == 0), 0, late_acc)
    odd_acc, even_acc, leaving = lax.optimization_barrier((odd_acc, even_acc, leaving))
    own_sum, queries_both = lax.optimization_barrier((own_sum, (first_query, second_query)))
    arrived = [across_chips(leaving[k - 1], k) for k in partners]
    arrived.insert(-1, section_swap(even_acc, 1))
    arrived.append(section_swap(odd_acc, 0))
    key_grads, value_grads = finished(first_acc, own_sum, arrived)
    query_grads = jnp.stack(queries_both, axis=0)[:, None]
    return (query_grads, key_grads, value_grads)


def solution(mesh):
    sections, ctx_count = mesh.shape["section"], mesh.shape["ctx"]
    chip_mesh = jax.sharding.Mesh(
        mesh.devices.reshape(sections, ctx_count // 2, 2), ("section", "z", "core")
    )
    tokens = ("z", "core")
    return jax.shard_map(
        body,
        mesh=chip_mesh,
        in_specs=(
            P(None, "section", tokens, None),
            P(None, "section", tokens, None),
            P("section", tokens, None),
            P("section", tokens, None),
            P(tokens, None),
            P(tokens, None),
            P("section", tokens, None),
            P("section", tokens, None),
            P(),
        ),
        out_specs=(
            P(None, "section", tokens, None),
            P(None, "section", tokens, None),
            P(None, "section", tokens, None),
        ),
        check_vma=False,
    )
```

```python
import math

import jax
import jax.numpy as jnp
from jax import lax
from jax.experimental import pallas as pl
from jax.experimental.pallas import tpu as pltpu
from jax.sharding import PartitionSpec as P

MASK_FILL = -1e30
STRIP = 32
CONTRACT_LAST = (((1,), (1,)), ((), ()))


def block_places(chips):
    return [(k, same) for same in (True, False) for k in range(chips)]


def stack_kernel(order_ref, q_ref, g_ref, q_out_ref, g_out_ref, cap_ref):
    ticks, _, local_rows, model = q_ref.shape
    head_dim = q_out_ref.shape[1]
    heads = model // head_dim
    for tick in range(ticks):
        for head in range(heads):
            rows = pl.ds((tick * heads + head) * local_rows, local_rows)
            cols = pl.ds(head * head_dim, head_dim)
            q_out_ref[rows, :] = q_ref[tick, 0, :, cols]
            g_out_ref[rows, :] = g_ref[tick, 0, :, cols]
    chip, core = lax.axis_index("z"), lax.axis_index("core")
    own_group = order_ref[2 * chip + core]
    for slot, (k, same) in enumerate(block_places(cap_ref.shape[0] // 16)):
        source = 2 * jnp.bitwise_xor(chip, k) + (core if same else 1 - core)
        cap = jnp.where(order_ref[source] <= own_group, -MASK_FILL, MASK_FILL)
        cap_ref[slot * 8 : (slot + 1) * 8, :] = jnp.full((8, cap_ref.shape[1]), cap, jnp.float32)


def stacked_heads(group_order, queries, out_grad, head_dim):
    rows = queries.size // head_dim
    in_vmem = pl.BlockSpec(memory_space=pltpu.VMEM)
    stack = jax.ShapeDtypeStruct((rows, head_dim), queries.dtype)
    caps = jax.ShapeDtypeStruct((8 * group_order.size, 2 * queries.shape[2]), jnp.float32)
    return pl.pallas_call(
        stack_kernel,
        out_shape=(stack, stack, caps),
        in_specs=[pl.BlockSpec(memory_space=pltpu.SMEM), in_vmem, in_vmem],
        out_specs=(in_vmem, in_vmem, in_vmem),
        compiler_params=pltpu.CompilerParams(vmem_limit_bytes=8 * 2**20),
        cost_estimate=pl.CostEstimate(
            flops=queries.size, bytes_accessed=8 * queries.size, transcendentals=0
        ),
    )(group_order, queries, out_grad)


def tick_kernel(tick, arrays, *refs):
    q_ref, g_ref, cap_ref = refs[:3]
    outs = refs[3 + arrays :]
    dq_ref, near_out_ref, far_out_ref, s_ref, e_ref, dp_ref, *more = outs
    p_ref, ds_ref, acc_ref, kt_ref = more
    local_rows, model = dq_ref.shape
    head_dim = near_out_ref.shape[1] // 2
    half_rows = near_out_ref.shape[0]
    kv_refs = [
        ref.at[pl.ds(row, local_rows)]
        for ref in refs[3 : 3 + arrays]
        for row in range(0, ref.shape[0], local_rows)
    ]
    blocks = len(kv_refs)
    heads = model // head_dim
    pairs = heads // 2
    width = 2 * local_rows
    chips = blocks // 2
    scale = 1.0 / math.sqrt(head_dim)
    exp_scale = scale * math.log2(math.e)

    for slot in range(blocks):
        kt_ref[:, slot * local_rows : (slot + 1) * local_rows] = kv_refs[slot][:, :head_dim].T

    def pair_of(ref, pair):
        return ref[pl.ds((tick * pairs + pair) * width, width), :]

    def rows_of(slot):
        return slice(slot * local_rows, (slot + 1) * local_rows)

    def products(pair, slot):
        for out, ref, lo in ((s_ref, q_ref, 0), (dp_ref, g_ref, head_dim)):
            out[pair, rows_of(slot)] = lax.dot_general(
                kv_refs[slot][:, lo : lo + head_dim],
                pair_of(ref, pair),
                CONTRACT_LAST,
                preferred_element_type=jnp.float32,
            )

    def strips(slot):
        first = slot * local_rows
        return [slice(row, row + STRIP) for row in range(first, first + local_rows, STRIP)]

    def folded(strip, combine):
        return combine(strip.reshape(STRIP // 8, 8, width), axis=0)

    def exponentials(pair, slot):
        top = jnp.full((8, width), MASK_FILL, jnp.float32)
        for rows in strips(slot):
            scores = s_ref[pair, rows]
            if slot == 0:
                key_row = rows.start + lax.broadcasted_iota(jnp.int32, (STRIP, width), 0)
                query_row = lax.rem(
                    lax.broadcasted_iota(jnp.int32, (STRIP, width), 1), local_rows
                )
                scores = jnp.where(key_row <= query_row, scores, MASK_FILL)
                s_ref[pair, rows] = scores
            top = jnp.maximum(top, folded(scores, jnp.max))
        peak = jnp.max(top, axis=0, keepdims=True) * exp_scale
        total = jnp.zeros((8, width), jnp.float32)
        weighted = jnp.zeros((8, width), jnp.float32)
        for rows in strips(slot):
            expo = jnp.exp2(s_ref[pair, rows] * exp_scale - peak)
            e_ref[pair, rows] = expo
            total += folded(expo, jnp.sum)
            weighted += folded(expo * dp_ref[pair, rows], jnp.sum)
        if slot > 0:
            peak = jnp.minimum(peak, cap_ref[8 * slot : 8 * slot + 1, :])
        return (
            peak,
            jnp.sum(total, axis=0, keepdims=True),
            jnp.sum(weighted, axis=0, keepdims=True),
        )

    def combined(parts):
        biggest = parts[0][0]
        for peak, _, _ in parts[1:]:
            biggest = jnp.maximum(biggest, peak)
        factors = [jnp.exp2(peak - biggest) for peak, _, _ in parts]
        total = sum(part[1] * factor for part, factor in zip(parts, factors))
        weighted = sum(part[2] * factor for part, factor in zip(parts, factors))
        inverse = 1.0 / total
        return [factor * inverse for factor in factors], weighted * inverse

    def gradients(pair, slot, factors, delta):
        for rows in strips(slot):
            probs = e_ref[pair, rows] * factors[slot]
            p_ref[pair, rows] = probs.astype(jnp.bfloat16)
            ds_ref[pair, rows] = (probs * (dp_ref[pair, rows] - delta)).astype(jnp.bfloat16)
        rows = rows_of(slot)
        key_terms = jnp.dot(
            ds_ref[pair, rows], pair_of(q_ref, pair), preferred_element_type=jnp.float32
        )
        value_terms = jnp.dot(
            p_ref[pair, rows], pair_of(g_ref, pair), preferred_element_type=jnp.float32
        )
        if pair > 0:
            key_terms += acc_ref[rows, :head_dim]
            value_terms += acc_ref[rows, head_dim:]
        if pair < pairs - 1:
            acc_ref[rows, :head_dim] = key_terms
            acc_ref[rows, head_dim:] = value_terms
        else:
            out = near_out_ref if slot < chips else far_out_ref
            place = rows_of(slot % chips)
            out[place, :head_dim] = (key_terms * scale).astype(out.dtype)
            out[place, head_dim:] = value_terms.astype(out.dtype)

    def query_grad(pair):
        query_t = jnp.dot(kt_ref[...], ds_ref[pair], preferred_element_type=jnp.float32)
        for half in range(2):
            lo = (2 * pair + half) * head_dim
            dq_ref[:, lo : lo + head_dim] = (
                query_t[:, half * local_rows : (half + 1) * local_rows].T * scale
            ).astype(dq_ref.dtype)

    held = None
    for pair in range(pairs + 1):
        parts = []
        if pair < pairs:
            products(pair, 0)
        for slot in range(blocks):
            if pair < pairs and slot + 1 < blocks:
                products(pair, slot + 1)
            if pair < pairs:
                parts.append(exponentials(pair, slot))
            if pair > 0:
                gradients(pair - 1, slot, *held)
            if pair > 1 and slot == 1:
                query_grad(pair - 2)
        if pair < pairs:
            held = combined(parts)
    query_grad(pairs - 1)


def attend_back(tick, queries, stacks, kv_arrays):
    local_rows, model = queries.shape[2:]
    width = kv_arrays[0].shape[1]
    key_rows = sum(array.shape[0] for array in kv_arrays)
    head_dim = width // 2
    pairs = model // head_dim // 2
    in_vmem = pl.BlockSpec(memory_space=pltpu.VMEM)
    tile = (pairs, key_rows, 2 * local_rows)

    def kernel(*refs):
        tick_kernel(tick, len(kv_arrays), *refs)

    return pl.pallas_call(
        kernel,
        out_shape=(
            jax.ShapeDtypeStruct((local_rows, model), jnp.bfloat16),
            jax.ShapeDtypeStruct((key_rows // 2, width), jnp.float32),
            jax.ShapeDtypeStruct((key_rows // 2, width), jnp.bfloat16),
        ),
        in_specs=[in_vmem] * (3 + len(kv_arrays)),
        out_specs=(in_vmem, in_vmem, in_vmem),
        scratch_shapes=[
            pltpu.VMEM(tile, jnp.float32),
            pltpu.VMEM(tile, jnp.float32),
            pltpu.VMEM(tile, jnp.float32),
            pltpu.VMEM(tile, jnp.bfloat16),
            pltpu.VMEM(tile, jnp.bfloat16),
            pltpu.VMEM((key_rows, width), jnp.float32),
            pltpu.VMEM((head_dim, key_rows), jnp.bfloat16),
        ],
        compiler_params=pltpu.CompilerParams(vmem_limit_bytes=44 * 2**20),
        cost_estimate=pl.CostEstimate(
            flops=40 * model * key_rows * local_rows,
            bytes_accessed=6 * local_rows * model + 5 * key_rows * width,
            transcendentals=model // head_dim * key_rows * local_rows,
        ),
    )(*stacks, *kv_arrays)


def other_core(block):
    return lax.ppermute(block, "core", [(0, 1), (1, 0)])


def across_chips(block, k):
    return lax.ppermute(block, "z", [(chip, chip ^ k) for chip in range(lax.axis_size("z"))])


def section_swap(block, first):
    sections = lax.axis_size("section")
    route = []
    for low in range(first, sections, 2):
        high = (low + 1) % sections
        route += [(low, high), (high, low)]
    return lax.ppermute(block, "section", route)


def body(
    queries,
    out_grad,
    keys,
    values,
    entering_keys,
    entering_values,
    key_grads_in,
    value_grads_in,
    group_order,
):
    local_rows, head_dim = keys.shape[1:]
    width = 2 * head_dim
    chips = lax.axis_size("z")
    sections = lax.axis_size("section")
    section = lax.axis_index("section")

    own_pair = jnp.concatenate([keys[0], values[0]], axis=1)
    entering_pair = jnp.concatenate([entering_keys, entering_values], axis=1)
    leaving_pair = jnp.where(section == 0, entering_pair, own_pair)

    partners = range(chips - 1, 0, -1)
    near = [across_chips(own_pair, k) for k in partners][::-1]
    own_far = other_core(own_pair)
    next_pair = lax.ppermute(
        leaving_pair, "section", [(i, (i - 1) % sections) for i in range(sections)]
    )
    stacks = stacked_heads(group_order, queries, out_grad, head_dim)
    near, next_pair, stacks = lax.optimization_barrier((near, next_pair, stacks))
    far = [own_far] + [other_core(block) for block in near]
    next_near = [across_chips(next_pair, k) for k in partners][::-1]
    first_query, near_terms, far_terms = attend_back(0, queries, stacks, [own_pair, *near, *far])
    *others, farthest = next_near
    far_terms, others, farthest, next_pair = lax.optimization_barrier(
        (far_terms, others[::-1], farthest, next_pair)
    )
    next_near = [next_pair, *others[::-1], farthest]
    next_kv = [*next_near, other_core(jnp.concatenate(next_near, axis=0))]

    def chip_sums(near_terms, far_terms):
        sums = near_terms + other_core(far_terms).astype(jnp.float32)
        sums = sums.reshape(chips, local_rows, width)
        return sums[0], [sums[k].astype(jnp.bfloat16) for k in range(1, chips)]

    def reduced(own_sum, leaving):
        for k in partners:
            own_sum = own_sum + across_chips(leaving[k - 1], k).astype(jnp.float32)
        return own_sum

    own_sum, leaving = chip_sums(near_terms, far_terms)
    stacks, leaving = lax.optimization_barrier((stacks, leaving))
    first_acc = jnp.concatenate([key_grads_in[0], value_grads_in[0]], axis=1) + reduced(
        own_sum, leaving
    )
    second_query, near_terms, far_terms = attend_back(1, queries, stacks, next_kv)
    first_acc, far_terms = lax.optimization_barrier((first_acc, far_terms))
    early_acc = section_swap(first_acc, 1)
    own_sum, leaving = chip_sums(near_terms, far_terms)
    late_acc, leaving = lax.optimization_barrier((first_acc.astype(jnp.bfloat16), leaving))
    own_sum, queries_both = lax.optimization_barrier((own_sum, (first_query, second_query)))
    second_acc = reduced(own_sum, leaving)
    late_acc = section_swap(late_acc, 0).astype(jnp.float32)
    moved_acc = jnp.where(section % 2 == 0, late_acc, early_acc)
    second_acc = second_acc + jnp.where(section == sections - 1, 0.0, moved_acc)
    query_grads = jnp.stack(queries_both, axis=0)[:, None]
    key_grads = jnp.stack([first_acc[:, :head_dim], second_acc[:, :head_dim]], axis=0)[:, None]
    value_grads = jnp.stack([first_acc[:, head_dim:], second_acc[:, head_dim:]], axis=0)[:, None]
    return (query_grads, key_grads, value_grads)


def solution(mesh):
    sections, ctx_count = mesh.shape["section"], mesh.shape["ctx"]
    chip_mesh = jax.sharding.Mesh(
        mesh.devices.reshape(sections, ctx_count // 2, 2), ("section", "z", "core")
    )
    tokens = ("z", "core")
    return jax.shard_map(
        body,
        mesh=chip_mesh,
        in_specs=(
            P(None, "section", tokens, None),
            P(None, "section", tokens, None),
            P("section", tokens, None),
            P("section", tokens, None),
            P(tokens, None),
            P(tokens, None),
            P("section", tokens, None),
            P("section", tokens, None),
            P(),
        ),
        out_specs=(
            P(None, "section", tokens, None),
            P(None, "section", tokens, None),
            P(None, "section", tokens, None),
        ),
        check_vma=False,
    )
```

```python
import math

import jax
import jax.numpy as jnp
from jax import lax
from jax.experimental import pallas as pl
from jax.experimental.pallas import tpu as pltpu
from jax.sharding import PartitionSpec as P

MASK_FILL = -1e30
STRIP = 32
CONTRACT_LAST = (((1,), (1,)), ((), ()))


def block_places(chips):
    return [(k, same) for same in (True, False) for k in range(chips)]


def stack_kernel(order_ref, q_ref, g_ref, q_out_ref, g_out_ref, cap_ref):
    ticks, _, local_rows, model = q_ref.shape
    head_dim = q_out_ref.shape[1]
    heads = model // head_dim
    for tick in range(ticks):
        for head in range(heads):
            rows = pl.ds((tick * heads + head) * local_rows, local_rows)
            cols = pl.ds(head * head_dim, head_dim)
            q_out_ref[rows, :] = q_ref[tick, 0, :, cols]
            g_out_ref[rows, :] = g_ref[tick, 0, :, cols]
    chip, core = lax.axis_index("z"), lax.axis_index("core")
    own_group = order_ref[2 * chip + core]
    for slot, (k, same) in enumerate(block_places(cap_ref.shape[0] // 16)):
        source = 2 * jnp.bitwise_xor(chip, k) + (core if same else 1 - core)
        cap = jnp.where(order_ref[source] <= own_group, -MASK_FILL, MASK_FILL)
        cap_ref[slot * 8 : (slot + 1) * 8, :] = jnp.full((8, cap_ref.shape[1]), cap, jnp.float32)


def stacked_heads(group_order, queries, out_grad, head_dim):
    rows = queries.size // head_dim
    in_vmem = pl.BlockSpec(memory_space=pltpu.VMEM)
    stack = jax.ShapeDtypeStruct((rows, head_dim), queries.dtype)
    caps = jax.ShapeDtypeStruct((8 * group_order.size, 2 * queries.shape[2]), jnp.float32)
    return pl.pallas_call(
        stack_kernel,
        out_shape=(stack, stack, caps),
        in_specs=[pl.BlockSpec(memory_space=pltpu.SMEM), in_vmem, in_vmem],
        out_specs=(in_vmem, in_vmem, in_vmem),
        compiler_params=pltpu.CompilerParams(vmem_limit_bytes=8 * 2**20),
        cost_estimate=pl.CostEstimate(
            flops=queries.size, bytes_accessed=8 * queries.size, transcendentals=0
        ),
    )(group_order, queries, out_grad)


def tick_kernel(tick, arrays, *refs):
    q_ref, g_ref, cap_ref = refs[:3]
    outs = refs[3 + arrays :]
    dq_ref, near_out_ref, far_out_ref, s_ref, e_ref, dp_ref, *more = outs
    p_ref, ds_ref, acc_ref, kt_ref = more
    local_rows, model = dq_ref.shape
    head_dim = near_out_ref.shape[1] // 2
    half_rows = near_out_ref.shape[0]
    kv_refs = [
        ref.at[pl.ds(row, local_rows)]
        for ref in refs[3 : 3 + arrays]
        for row in range(0, ref.shape[0], local_rows)
    ]
    blocks = len(kv_refs)
    heads = model // head_dim
    pairs = heads // 2
    width = 2 * local_rows
    chips = blocks // 2
    scale = 1.0 / math.sqrt(head_dim)
    exp_scale = scale * math.log2(math.e)

    for slot in range(blocks):
        kt_ref[:, slot * local_rows : (slot + 1) * local_rows] = kv_refs[slot][:, :head_dim].T

    def pair_of(ref, pair):
        return ref[pl.ds((tick * pairs + pair) * width, width), :]

    def rows_of(slot):
        return slice(slot * local_rows, (slot + 1) * local_rows)

    def products(pair, slot):
        for out, ref, lo in ((s_ref, q_ref, 0), (dp_ref, g_ref, head_dim)):
            out[pair, rows_of(slot)] = lax.dot_general(
                kv_refs[slot][:, lo : lo + head_dim],
                pair_of(ref, pair),
                CONTRACT_LAST,
                preferred_element_type=jnp.float32,
            )

    def strips(slot):
        first = slot * local_rows
        return [slice(row, row + STRIP) for row in range(first, first + local_rows, STRIP)]

    def folded(strip, combine):
        return combine(strip.reshape(STRIP // 8, 8, width), axis=0)

    def exponentials(pair, slot):
        top = jnp.full((8, width), MASK_FILL, jnp.float32)
        for rows in strips(slot):
            scores = s_ref[pair, rows]
            if slot == 0:
                key_row = rows.start + lax.broadcasted_iota(jnp.int32, (STRIP, width), 0)
                query_row = lax.rem(
                    lax.broadcasted_iota(jnp.int32, (STRIP, width), 1), local_rows
                )
                scores = jnp.where(key_row <= query_row, scores, MASK_FILL)
                s_ref[pair, rows] = scores
            top = jnp.maximum(top, folded(scores, jnp.max))
        peak = jnp.max(top, axis=0, keepdims=True) * exp_scale
        total = jnp.zeros((8, width), jnp.float32)
        weighted = jnp.zeros((8, width), jnp.float32)
        for rows in strips(slot):
            expo = jnp.exp2(s_ref[pair, rows] * exp_scale - peak)
            e_ref[pair, rows] = expo
            total += folded(expo, jnp.sum)
            weighted += folded(expo * dp_ref[pair, rows], jnp.sum)
        if slot > 0:
            peak = jnp.minimum(peak, cap_ref[8 * slot : 8 * slot + 1, :])
        return (
            peak,
            jnp.sum(total, axis=0, keepdims=True),
            jnp.sum(weighted, axis=0, keepdims=True),
        )

    def combined(parts):
        biggest = parts[0][0]
        for peak, _, _ in parts[1:]:
            biggest = jnp.maximum(biggest, peak)
        factors = [jnp.exp2(peak - biggest) for peak, _, _ in parts]
        total = sum(part[1] * factor for part, factor in zip(parts, factors))
        weighted = sum(part[2] * factor for part, factor in zip(parts, factors))
        inverse = 1.0 / total
        return [factor * inverse for factor in factors], weighted * inverse

    def gradients(pair, slot, factors, delta):
        for rows in strips(slot):
            probs = e_ref[pair, rows] * factors[slot]
            p_ref[pair, rows] = probs.astype(jnp.bfloat16)
            ds_ref[pair, rows] = (probs * (dp_ref[pair, rows] - delta)).astype(jnp.bfloat16)
        rows = rows_of(slot)
        key_terms = jnp.dot(
            ds_ref[pair, rows], pair_of(q_ref, pair), preferred_element_type=jnp.float32
        )
        value_terms = jnp.dot(
            p_ref[pair, rows], pair_of(g_ref, pair), preferred_element_type=jnp.float32
        )
        if pair > 0:
            key_terms += acc_ref[rows, :head_dim]
            value_terms += acc_ref[rows, head_dim:]
        if pair < pairs - 1:
            acc_ref[rows, :head_dim] = key_terms
            acc_ref[rows, head_dim:] = value_terms
        else:
            out = near_out_ref if slot < chips else far_out_ref
            place = rows_of(slot % chips)
            out[place, :head_dim] = (key_terms * scale).astype(out.dtype)
            out[place, head_dim:] = value_terms.astype(out.dtype)

    def query_grad(pair):
        query_t = jnp.dot(kt_ref[...], ds_ref[pair], preferred_element_type=jnp.float32)
        for half in range(2):
            lo = (2 * pair + half) * head_dim
            dq_ref[:, lo : lo + head_dim] = (
                query_t[:, half * local_rows : (half + 1) * local_rows].T * scale
            ).astype(dq_ref.dtype)

    held = None
    for pair in range(pairs + 1):
        parts = []
        if pair < pairs:
            products(pair, 0)
        for slot in range(blocks):
            if pair < pairs and slot + 1 < blocks:
                products(pair, slot + 1)
            if pair < pairs:
                parts.append(exponentials(pair, slot))
            if pair > 0:
                gradients(pair - 1, slot, *held)
            if pair > 1 and slot == 1:
                query_grad(pair - 2)
        if pair < pairs:
            held = combined(parts)
    query_grad(pairs - 1)


def attend_back(tick, queries, stacks, kv_arrays):
    local_rows, model = queries.shape[2:]
    width = kv_arrays[0].shape[1]
    key_rows = sum(array.shape[0] for array in kv_arrays)
    head_dim = width // 2
    pairs = model // head_dim // 2
    in_vmem = pl.BlockSpec(memory_space=pltpu.VMEM)
    tile = (pairs, key_rows, 2 * local_rows)

    def kernel(*refs):
        tick_kernel(tick, len(kv_arrays), *refs)

    return pl.pallas_call(
        kernel,
        out_shape=(
            jax.ShapeDtypeStruct((local_rows, model), jnp.bfloat16),
            jax.ShapeDtypeStruct((key_rows // 2, width), jnp.float32),
            jax.ShapeDtypeStruct((key_rows // 2, width), jnp.bfloat16),
        ),
        in_specs=[in_vmem] * (3 + len(kv_arrays)),
        out_specs=(in_vmem, in_vmem, in_vmem),
        scratch_shapes=[
            pltpu.VMEM(tile, jnp.float32),
            pltpu.VMEM(tile, jnp.float32),
            pltpu.VMEM(tile, jnp.float32),
            pltpu.VMEM(tile, jnp.bfloat16),
            pltpu.VMEM(tile, jnp.bfloat16),
            pltpu.VMEM((key_rows, width), jnp.float32),
            pltpu.VMEM((head_dim, key_rows), jnp.bfloat16),
        ],
        compiler_params=pltpu.CompilerParams(vmem_limit_bytes=44 * 2**20),
        cost_estimate=pl.CostEstimate(
            flops=40 * model * key_rows * local_rows,
            bytes_accessed=6 * local_rows * model + 5 * key_rows * width,
            transcendentals=model // head_dim * key_rows * local_rows,
        ),
    )(*stacks, *kv_arrays)


def finish_kernel(first_ref, own_ref, *refs):
    key_ref, value_ref, held, copy_sem = refs[-4:]
    head_dim = key_ref.shape[3]
    copies = []
    for tick in range(2):
        total = (first_ref if tick == 0 else own_ref)[...]
        if tick == 1:
            for ref in refs[:-4]:
                total = total + ref[...].astype(jnp.float32)
        for half, out in enumerate((key_ref, value_ref)):
            held[tick, half] = total[:, half * head_dim : (half + 1) * head_dim]
            copy = pltpu.make_async_copy(
                held.at[tick, half], out.at[tick, 0], copy_sem.at[2 * tick + half]
            )
            copy.start()
            copies.append(copy)
    for copy in copies:
        copy.wait()


def finished(first_acc, own_sum, blocks):
    rows, width = first_acc.shape
    head_dim = width // 2
    in_vmem = pl.BlockSpec(memory_space=pltpu.VMEM)
    return pl.pallas_call(
        finish_kernel,
        out_shape=(jax.ShapeDtypeStruct((2, 1, rows, head_dim), jnp.float32),) * 2,
        in_specs=[in_vmem] * (2 + len(blocks)),
        out_specs=(pl.BlockSpec(memory_space=pl.ANY),) * 2,
        scratch_shapes=[
            pltpu.VMEM((2, 2, rows, head_dim), jnp.float32),
            pltpu.SemaphoreType.DMA((4,)),
        ],
        compiler_params=pltpu.CompilerParams(vmem_limit_bytes=8 * 2**20),
        cost_estimate=pl.CostEstimate(
            flops=len(blocks) * first_acc.size,
            bytes_accessed=16 * first_acc.size,
            transcendentals=0,
        ),
    )(first_acc, own_sum, *blocks)


def other_core(block):
    return lax.ppermute(block, "core", [(0, 1), (1, 0)])


def across_chips(block, k):
    return lax.ppermute(block, "z", [(chip, chip ^ k) for chip in range(lax.axis_size("z"))])


def section_swap(block, first):
    sections = lax.axis_size("section")
    route = []
    for low in range(first, sections, 2):
        high = (low + 1) % sections
        route += [(low, high), (high, low)]
    return lax.ppermute(block, "section", route)


def body(
    queries,
    out_grad,
    keys,
    values,
    entering_keys,
    entering_values,
    key_grads_in,
    value_grads_in,
    group_order,
):
    local_rows, head_dim = keys.shape[1:]
    width = 2 * head_dim
    chips = lax.axis_size("z")
    sections = lax.axis_size("section")
    section = lax.axis_index("section")

    own_pair = jnp.concatenate([keys[0], values[0]], axis=1)
    entering_pair = jnp.concatenate([entering_keys, entering_values], axis=1)
    leaving_pair = jnp.where(section == 0, entering_pair, own_pair)

    partners = range(chips - 1, 0, -1)
    near = [across_chips(own_pair, k) for k in partners][::-1]
    own_far = other_core(own_pair)
    next_pair = lax.ppermute(
        leaving_pair, "section", [(i, (i - 1) % sections) for i in range(sections)]
    )
    stacks = stacked_heads(group_order, queries, out_grad, head_dim)
    near, next_pair, stacks = lax.optimization_barrier((near, next_pair, stacks))
    far = [own_far] + [other_core(block) for block in near]
    next_near = [across_chips(next_pair, k) for k in partners][::-1]
    first_query, near_terms, far_terms = attend_back(0, queries, stacks, [own_pair, *near, *far])
    *others, farthest = next_near
    far_terms, others, farthest, next_pair = lax.optimization_barrier(
        (far_terms, others[::-1], farthest, next_pair)
    )
    next_near = [next_pair, *others[::-1], farthest]
    next_kv = [*next_near, other_core(jnp.concatenate(next_near, axis=0))]

    def chip_sums(near_terms, received):
        sums = near_terms + received.astype(jnp.float32)
        sums = sums.reshape(chips, local_rows, width)
        return sums[0], [sums[k].astype(jnp.bfloat16) for k in range(1, chips)]

    def reduced(own_sum, leaving):
        for k in partners:
            own_sum = own_sum + across_chips(leaving[k - 1], k).astype(jnp.float32)
        return own_sum

    own_sum, leaving = chip_sums(near_terms, other_core(far_terms))
    stacks, leaving = lax.optimization_barrier((stacks, leaving))
    first_acc = jnp.concatenate([key_grads_in[0], value_grads_in[0]], axis=1) + reduced(
        own_sum, leaving
    )
    second_query, near_terms, far_terms = attend_back(1, queries, stacks, next_kv)
    received = other_core(far_terms)
    first_acc, received = lax.optimization_barrier((first_acc, received))
    own_sum, leaving = chip_sums(near_terms, received)
    is_odd = section % 2 == 1
    late_acc = first_acc.astype(jnp.bfloat16)
    odd_acc = jnp.where(is_odd, late_acc, 0)
    even_acc = jnp.where(is_odd | (section == 0), 0, late_acc)
    odd_acc, even_acc, leaving = lax.optimization_barrier((odd_acc, even_acc, leaving))
    own_sum, queries_both = lax.optimization_barrier((own_sum, (first_query, second_query)))
    arrived = [across_chips(leaving[k - 1], k) for k in partners]
    arrived.append(section_swap(even_acc, 1))
    arrived.append(section_swap(odd_acc, 0))
    key_grads, value_grads = finished(first_acc, own_sum, arrived)
    query_grads = jnp.stack(queries_both, axis=0)[:, None]
    return (query_grads, key_grads, value_grads)


def solution(mesh):
    sections, ctx_count = mesh.shape["section"], mesh.shape["ctx"]
    chip_mesh = jax.sharding.Mesh(
        mesh.devices.reshape(sections, ctx_count // 2, 2), ("section", "z", "core")
    )
    tokens = ("z", "core")
    return jax.shard_map(
        body,
        mesh=chip_mesh,
        in_specs=(
            P(None, "section", tokens, None),
            P(None, "section", tokens, None),
            P("section", tokens, None),
            P("section", tokens, None),
            P(tokens, None),
            P(tokens, None),
            P("section", tokens, None),
            P("section", tokens, None),
            P(),
        ),
        out_specs=(
            P(None, "section", tokens, None),
            P(None, "section", tokens, None),
            P(None, "section", tokens, None),
        ),
        check_vma=False,
    )
```
